512 devices in a mesh: dp: 64 (over y, z_lo, core), score: 8 (over z_hi, x).
Axes of the slice: x: 4, y: 4, z: 16 (z_hi: 2, z_lo: 8; z = z_hi * 8 + z_lo), core: 2. Of those that a mesh axis runs over, the one named last changes fastest.
Arguments:
- hidden_in: bfloat16 [65536, 8192], P(('score', 'dp')), may hold values from -30 to 30
- norm_gain: float32 [8192], replicated, may hold values from 0.1 to 1.9
- value_weight: bfloat16 [8192, 512], P('dp'), may hold values from -0.0625 to 0.0625
- input_proj: bfloat16 [8192, 64], P('dp'), may hold values from -0.0625 to 0.0625
- value_grad: bfloat16 [65536, 512], P(('score', 'dp')), may hold values from -6 to 6
- output_proj: bfloat16 [512, 64], replicated, may hold values from -0.25 to 0.25
- doc_ids: int32 [65536], P(('score', 'dp')), may hold values from 0 to 63, as said below
- queries: bfloat16 [8192, 4096], P(('dp', 'score')), may hold values from -0.0020599365 to 0.0020599365
Outputs:
- values_out: bfloat16 [65536, 512], P(('score', 'dp'))
- hidden_grad: bfloat16 [65536, 8192], P(('score', 'dp'))
- scores: float32 [64, 8192], P('score', 'dp')
The draws below stay inside these ranges and needn't reach their ends.
Inputs may be any that keep to these rules, and one draw needn't show every extreme that they name: `doc_ids`: document numbers never fall along the tokens; every document holds 1 to 8192 tokens and one holds exactly 8192.
All inputs are finite; a program needn't handle non-finite values.
Results may differ from the reference program's by a relative error of at most 0.0049.
Values may be sent and summed in bfloat16 or wider, within the bound.
No kernel may reach another device: no remote copies, remote signals or barrier semaphores. Data moves between devices by JAX's collectives and lax.ppermute only.
A program may use at most 64 MiB of HBM per device.

```python
import jax
import jax.numpy as jnp
from jax import lax

D = 8192
KV_W = 512
RANK = 64
TOK_DEV = 128
TOKENS = 65536
DOCS = 64
DOC_MAX = 8192
QUERIES = 8192


def draw_hidden_in(key, part):
    key = jax.random.fold_in(key, 7)
    key_base, key_rows, key_cols = jax.random.split(key, 3)
    row_scale = jnp.exp(jax.random.uniform(key_rows, (TOKENS, 1), jnp.float32, 0.0, jnp.log(10.0)))
    col_scale = jnp.exp(jax.random.uniform(key_cols, (1, D), jnp.float32, 0.0, jnp.log(10.0)))
    base = jnp.clip(jax.random.normal(key_base, (TOKENS, D), jnp.float32), -6.0, 6.0)
    return (0.05 * base * row_scale * col_scale).astype(jnp.bfloat16)


def draw_doc_ids(key, part):
    key = jax.random.fold_in(key, 11)
    key_short, key_weight, key_roll, key_place = jax.random.split(key, 4)
    short_count = max(1, DOCS // 4)
    long_count = DOCS - 1 - short_count
    short_len = jax.random.randint(key_short, (short_count,), 1, TOK_DEV // 4 + 1, jnp.int32)
    long_total = TOKENS - DOC_MAX - jnp.sum(short_len, dtype=jnp.int32)
    weights = jax.random.randint(key_weight, (long_count,), 1, 4, jnp.int32)
    cum_weight = jnp.concatenate([jnp.zeros((1,), jnp.int32), jnp.cumsum(weights, dtype=jnp.int32)])
    bounds = long_total * cum_weight // cum_weight[-1]
    long_len = (bounds[1:] - bounds[:-1]).astype(jnp.int32)
    head = jnp.concatenate([long_len, jnp.full((1,), DOC_MAX, jnp.int32)])
    roll_by = jax.random.randint(key_roll, (), 0, long_count + 1, jnp.int32)
    head = jnp.roll(head, roll_by)
    canon = jnp.concatenate([head, short_len]).astype(jnp.int32)
    place = jax.random.randint(key_place, (), 0, long_count + 2, jnp.int32)
    slot = jnp.arange(DOCS, dtype=jnp.int32)
    order = jnp.where(slot < place, slot, jnp.where(slot < place + short_count, long_count + 1 + slot - place, slot - short_count)).astype(jnp.int32)
    lengths = canon[order]
    ends = jnp.cumsum(lengths, dtype=jnp.int32)
    positions = jnp.arange(TOKENS, dtype=jnp.int32)
    return jnp.sum((positions[:, None] >= ends[None, :]).astype(jnp.int32), axis=1, dtype=jnp.int32)


def level_of(stream_key, dims, pieces, smallest, high):
    def one(dim, shards_of):
        draws = jax.random.uniform(jax.random.fold_in(jax.random.fold_in(stream_key, 6), dim), (shards_of,), jnp.float32, smallest / len(pieces), high / len(pieces))
        return jnp.repeat(jnp.exp(draws), dims[dim] // shards_of).reshape((-1,) + (1,) * (len(dims) - dim - 1))

    level = one(*pieces[0])
    for cut in pieces[1:]:
        level = level * one(*cut)
    return level


def scatter_about(rng, dims, scale, reach, pieces=(), kind=jnp.bfloat16):
    array = jax.random.normal(rng, dims, jnp.float32) * scale
    if len(pieces) > 0:
        array = level_of(rng, dims, pieces, -0.22, 0.18) * array
    return jnp.clip(array, min=-reach, max=reach).astype(kind)


def setup_inputs(seed: int = 0) -> dict:
    arg_keys = jax.random.split(jax.random.key(seed), 9)
    return {
        "hidden_in": draw_hidden_in(jax.random.fold_in(arg_keys[8], 71), 0),
        "norm_gain": jnp.clip(1.0 + 0.18 * jax.random.normal(arg_keys[1], (D,), jnp.float32), 0.1, 1.9),
        "value_weight": scatter_about(arg_keys[2], (D, KV_W), D ** -0.5, 0.0625, ((0, 64),)),
        "input_proj": scatter_about(arg_keys[3], (D, RANK), D ** -0.5, 0.0625, ((0, 64),)),
        "value_grad": scatter_about(arg_keys[4], (TOKENS, KV_W), 1.0, 6.0, ((0, 512),)),
        "output_proj": scatter_about(arg_keys[5], (KV_W, RANK), KV_W ** -0.5, 0.25),
        "doc_ids": draw_doc_ids(jax.random.fold_in(arg_keys[8], 71), 0),
        "queries": scatter_about(arg_keys[7], (QUERIES, RANK * RANK), (2.0 / (RANK * (DOC_MAX ** 0.5))), 0.0020599365, ((0, 512),)),
    }


EPSILON = 1e-05

def reference(hidden_in, norm_gain, value_weight, input_proj, value_grad, output_proj, doc_ids, queries):
    block_size = TOK_DEV * 16
    block_count = TOKENS // block_size
    x_blocks = hidden_in.reshape(block_count, block_size, D)
    g_blocks = value_grad.reshape(block_count, block_size, KV_W)
    id_blocks = doc_ids.reshape(block_count, block_size)
    gain_vec = norm_gain.astype(jnp.float32)
    doc_range = jnp.arange(DOCS, dtype=jnp.int32)

    def block_step(total, block_items):
        block_x, block_g, block_ids = block_items
        wide_in = block_x.astype(jnp.float32)
        inv_rms = lax.rsqrt(lax.optimization_barrier(jnp.mean(wide_in * wide_in, axis=1, keepdims=True)) + EPSILON)
        normed = (wide_in * inv_rms * gain_vec).astype(jnp.bfloat16)
        values = jnp.dot(normed, value_weight, preferred_element_type=jnp.float32).astype(jnp.bfloat16)
        grad_normed = lax.dot_general(block_g, value_weight, (((1,), (1,)), ((), ())), preferred_element_type=jnp.float32) * gain_vec
        inner_sum = lax.optimization_barrier(jnp.mean(grad_normed * wide_in, axis=1, keepdims=True))
        cube = inv_rms * inv_rms * inv_rms
        grad_x = (inv_rms * grad_normed - wide_in * cube * inner_sum).astype(jnp.bfloat16)
        left_proj = jnp.dot(normed, input_proj, preferred_element_type=jnp.float32)
        right_proj = jnp.dot(block_g, output_proj, preferred_element_type=jnp.float32)
        onehot = (block_ids[:, None] == doc_range[None, :]).astype(jnp.float32)
        spread = (onehot[:, :, None] * left_proj[:, None, :]).reshape(block_size, DOCS * RANK)
        doc_term = jnp.dot(spread.T, right_proj, precision=lax.Precision.HIGHEST).reshape(DOCS, RANK * RANK)
        return (total + doc_term, (values, grad_x))
    initial = jnp.zeros((DOCS, RANK * RANK), jnp.float32)
    doc_grads, (values, grad_x) = lax.scan(block_step, initial, (x_blocks, g_blocks, id_blocks))
    doc_low = doc_grads.astype(jnp.bfloat16)
    scores = lax.dot_general(doc_low, queries, (((1,), (1,)), ((), ())), preferred_element_type=jnp.float32)
    return (values.reshape(TOKENS, KV_W), grad_x.reshape(TOKENS, D), scores)
```

```python
import jax
import jax.numpy as jnp
from jax import lax
from jax.sharding import Mesh
from jax.sharding import PartitionSpec as P

EPSILON = 1e-05
DP = ("y", "zl", "core")
SCORE = ("zh", "x")


def spread_to_all(value, axes):
    count = lax.axis_size(axes)
    copies = jnp.broadcast_to(value[None], (count,) + value.shape)
    return lax.all_to_all(copies, axes, 0, 0, tiled=True)


def swapped(value, axis):
    return lax.ppermute(value, axis, [(0, 1), (1, 0)])


def contract_last(left_side, right_side):
    return lax.dot_general(
        left_side, right_side, (((1,), (1,)), ((), ())), preferred_element_type=jnp.float32
    )


def ordered(first, own, other):
    return jnp.where(first, own, other), jnp.where(first, other, own)


def shards(
    hidden_in, norm_gain, value_weight, input_proj, value_grad, output_proj, doc_ids, queries
):
    rows, width = hidden_in.shape
    kv = value_weight.shape[1]
    rank = input_proj.shape[1]
    core = lax.axis_index("core")
    x_index = lax.axis_index("x")
    on_first = core == 0

    p_own = spread_to_all(spread_to_all(input_proj.T, "zl"), "y")
    p_other = swapped(p_own, "core")

    q_pair = jnp.stack([queries, swapped(queries, "zh")])
    q_all = spread_to_all(q_pair, "x")

    quarter = lax.dynamic_slice_in_dim(value_weight, x_index * (kv // 4), kv // 4, 1)
    w_z = spread_to_all(quarter, "zl")
    half = w_z.shape[0] // 2
    wa = spread_to_all(w_z[:half], "x").transpose(1, 2, 0, 3).reshape(half, -1, kv)
    wa = spread_to_all(wa, "y").reshape(-1, kv)
    wb = spread_to_all(spread_to_all(w_z[half:], "y"), "x")
    wb = wb.transpose(1, 2, 3, 0, 4).reshape(-1, kv)
    w_parts = (wa, wb, swapped(wa, "core"), swapped(wb, "core"))

    def cut(array):
        blocks = array.reshape(array.shape[0], 4, 2, half, 2, 128)
        parts = []
        for side in (core, 1 - core):
            mine = lax.dynamic_index_in_dim(blocks, side, 4, keepdims=False)
            for zone in range(2):
                parts.append(mine[:, :, zone].reshape(array.shape[0], -1))
        return parts

    wide_in = hidden_in.astype(jnp.float32)
    inv_rms = lax.rsqrt(jnp.mean(wide_in * wide_in, axis=1, keepdims=True) + EPSILON)
    normed = (wide_in * inv_rms * norm_gain).astype(jnp.bfloat16)

    right_t = lax.dot_general(
        output_proj, value_grad, (((0,), (1,)), ((), ())), preferred_element_type=jnp.float32
    )
    ids_row = jnp.broadcast_to(doc_ids.astype(jnp.float32)[None], (8, rows))
    right_all = spread_to_all(jnp.concatenate([right_t, ids_row], 0), ("y", "core"))
    p_first, p_second = ordered(on_first, p_own, p_other)
    p_full = jnp.stack([p_first, p_second], 2).reshape(64, rank, 128)
    p_full = p_full.transpose(1, 0, 2).reshape(rank, width)
    left_t = contract_last(p_full, normed)
    left_blocks = left_t.reshape(4, 8, 2, rows).transpose(0, 2, 1, 3).reshape(8, 8, rows)
    left_all = lax.all_to_all(left_blocks, ("y", "core"), 0, 0, tiled=True)

    doc_count = 64
    ids_all = right_all[:, rank].reshape(1, -1)
    right_flat = right_all[:, :rank].transpose(1, 0, 2).reshape(rank, -1)
    left_flat = left_all.transpose(1, 0, 2).reshape(8, 1, -1)
    doc_range = jnp.arange(doc_count, dtype=jnp.float32)[:, None]
    onehot = (ids_all == doc_range).astype(jnp.float32)
    spread = (onehot[None] * left_flat).reshape(8 * doc_count, -1)
    doc_term = lax.dot_general(
        spread, right_flat, (((1,), (1,)), ((), ())), precision=lax.Precision.HIGHEST
    )
    doc_term = doc_term.reshape(16, 2, 16, rank)
    doc_term = jnp.concatenate([doc_term[:, 0], doc_term[:, 1]], -1)
    z_parts = lax.all_to_all(doc_term, ("zl", "zh"), 0, 0, tiled=True)
    z_sum = jnp.sum(z_parts, 0)
    z_sum = jnp.concatenate([z_sum[:, :rank], z_sum[:, rank:]], 0).reshape(4, 8, rank)
    x_parts = lax.all_to_all(z_sum, "x", 0, 0, tiled=True)
    own_docs = jnp.sum(x_parts, 0).astype(jnp.bfloat16)
    doc_low = spread_to_all(own_docs, DP)
    doc_low = doc_low.transpose(1, 0, 2).reshape(8, -1)
    q_flat = q_all.reshape(-1, q_all.shape[-1])
    piece = contract_last(doc_low, q_flat).reshape(8, 4, 2, -1)
    first, second = ordered(lax.axis_index("zh") == 0, piece[:, :, 0], piece[:, :, 1])
    scores = jnp.concatenate([first.reshape(8, -1), second.reshape(8, -1)], 1)

    values_acc = jnp.zeros((rows, kv), jnp.float32)
    grads = []
    for normed_part, w_part in zip(cut(normed), w_parts):
        values_acc += jnp.dot(normed_part, w_part, preferred_element_type=jnp.float32)
        grads.append(contract_last(value_grad, w_part))
    values_out = values_acc.astype(jnp.bfloat16)
    along = jnp.sum(values_acc * value_grad.astype(jnp.float32), axis=1, keepdims=True)
    scale = inv_rms * inv_rms * along / width
    shape = (rows, 4, half, 128)
    own = jnp.stack([grads[0].reshape(shape), grads[1].reshape(shape)], 2)
    other = jnp.stack([grads[2].reshape(shape), grads[3].reshape(shape)], 2)
    grad_normed = jnp.stack(ordered(on_first, own, other), 4).reshape(rows, width) * norm_gain
    hidden_grad = (inv_rms * grad_normed - wide_in * scale).astype(jnp.bfloat16)
    return (values_out, hidden_grad, scores)


def solution(mesh):
    fine = Mesh(mesh.devices.reshape(4, 8, 2, 2, 4), DP + SCORE)
    tokens = SCORE + DP
    placed = (
        P(tokens, None),
        P(),
        P(DP, None),
        P(DP, None),
        P(tokens, None),
        P(),
        P(tokens),
        P(DP + SCORE, None),
    )
    return jax.shard_map(
        shards,
        mesh=fine,
        in_specs=placed,
        out_specs=(P(tokens, None), P(tokens, None), P(SCORE, DP)),
        check_vma=False,
    )
```

```python
import jax
import jax.numpy as jnp
from jax import lax
from jax.experimental import pallas as pl
from jax.experimental.pallas import tpu as pltpu
from jax.sharding import Mesh
from jax.sharding import PartitionSpec as P

EPSILON = 1e-05
DP = ("y", "zl", "core")
SCORE = ("zh", "x")
Y_STEPS = (0, 1, -1, 2)
Z_STEPS = (-1, 0, 1, 2, 3, 4, -3, -2)
BLOCK = 128
LIMIT = 48 * 1024 * 1024


def spread_to_all(value, axes):
    count = lax.axis_size(axes)
    copies = jnp.broadcast_to(value[None], (count,) + value.shape)
    return lax.all_to_all(copies, axes, 0, 0, tiled=True)


def swapped(value, axis):
    return lax.ppermute(value, axis, [(0, 1), (1, 0)])


def from_y(value, step):
    return lax.ppermute(value, "y", [((y + step) % 4, y) for y in range(4)])


def from_z(value, step):
    def place(z):
        return (z % 8) * 2 + z // 8

    return lax.ppermute(
        value, ("zl", "zh"), [(place((z + step) % 16), place(z)) for z in range(16)]
    )


def contract_last(left_side, right_side):
    return lax.dot_general(
        left_side, right_side, (((1,), (1,)), ((), ())), preferred_element_type=jnp.float32
    )


def ordered(first, own, other):
    return jnp.where(first, own, other), jnp.where(first, other, own)


def after(value, earlier):
    return lax.optimization_barrier((value, earlier))[0]


def left_kernel(core_ref, normed_ref, own_ref, other_ref, left_ref):
    first = core_ref[0] == 0
    rank = left_ref.shape[0]
    total = jnp.zeros(left_ref.shape, jnp.float32)
    for pair in range(32):
        y, z = divmod(pair, 8)
        own = own_ref[y, z * rank : (z + 1) * rank]
        other = other_ref[y, z * rank : (z + 1) * rank]
        factor = jnp.concatenate(ordered(first, own, other), 1)
        total += contract_last(factor, normed_ref[:, pair * 256 : (pair + 1) * 256])
    left_ref[...] = total


def layer_kernel(
    core_ref, place_ref, normed_ref, hidden_ref, gain_ref, scale_ref, grad_ref, own_ref, other_ref,
    values_ref, hidden_grad_ref,
):
    first = core_ref[0] == 0
    width = normed_ref.shape[1]
    grad = grad_ref[...]
    inv_rms = scale_ref[...]

    def weights(pair):
        rows = slice(pair * BLOCK, (pair + 1) * BLOCK)
        return jnp.concatenate(ordered(first, own_ref[rows], other_ref[rows]), 0)

    def columns(pair):
        return pl.ds(pl.multiple_of(place_ref[pair] * 256, 256), 256)

    total = jnp.zeros(values_ref.shape, jnp.float32)
    for pair in range(32):
        total += jnp.dot(
            normed_ref[:, columns(pair)], weights(pair), preferred_element_type=jnp.float32
        )
    values_ref[...] = total.astype(jnp.bfloat16)
    along = jnp.sum(total * grad.astype(jnp.float32), axis=1, keepdims=True)
    pull = inv_rms * inv_rms * along / width
    for pair in range(32):
        where = columns(pair)
        back = contract_last(grad, weights(pair)) * gain_ref[:, where]
        wide = hidden_ref[:, where].astype(jnp.float32)
        hidden_grad_ref[:, where] = (inv_rms * back - wide * pull).astype(jnp.bfloat16)


def shards(
    hidden_in, norm_gain, value_weight, input_proj, value_grad, output_proj, doc_ids, queries
):
    rows, width = hidden_in.shape
    kv = value_weight.shape[1]
    rank = input_proj.shape[1]
    core = lax.axis_index("core")
    core_row = core.astype(jnp.int32).reshape(1)
    on_first = core == 0
    smem = pl.BlockSpec(memory_space=pltpu.SMEM)
    vmem = pl.BlockSpec(memory_space=pltpu.VMEM)
    params = pltpu.CompilerParams(vmem_limit_bytes=LIMIT)

    factor = input_proj.T.reshape(4, 8, 2, BLOCK).transpose(0, 2, 1, 3).reshape(rank, BLOCK)
    right_t = lax.dot_general(
        output_proj, value_grad, (((0,), (1,)), ((), ())), preferred_element_type=jnp.float32
    )
    right_high = right_t.astype(jnp.bfloat16)
    right_low = (right_t - right_high.astype(jnp.float32)).astype(jnp.bfloat16)
    ids_rows = jnp.broadcast_to(doc_ids.astype(jnp.bfloat16)[None], (16, rows))
    factor_z = spread_to_all(factor, "zl").reshape(-1, BLOCK)
    packed = jnp.concatenate([factor_z, right_high, right_low, ids_rows], 0)
    packed = spread_to_all(packed, "y")
    packed_other = swapped(packed, "core")

    ahead, behind = from_z(value_weight, 1), from_z(value_weight, -1)
    near = after(jnp.concatenate([behind, value_weight, ahead], 0), factor_z)
    far_ahead, far_behind = from_z(near, 3), from_z(near[BLOCK:], -3)
    w_z = after(jnp.concatenate([near, far_ahead, far_behind], 0), packed)
    half = w_z.shape[0] // 2
    y_ahead, y_behind = from_y(w_z, 1), from_y(w_z, -1)

    q_all = lax.all_gather(queries, SCORE, axis=0, tiled=True)

    wide_in = hidden_in.astype(jnp.float32)
    inv_rms = lax.rsqrt(jnp.mean(wide_in * wide_in, axis=1, keepdims=True) + EPSILON)
    normed = (wide_in * inv_rms * norm_gain).astype(jnp.bfloat16)

    left_t = pl.pallas_call(
        left_kernel,
        out_shape=jax.ShapeDtypeStruct((rank, rows), jnp.float32),
        in_specs=[smem, vmem, vmem, vmem],
        out_specs=vmem,
        compiler_params=params,
        name="left_factor",
    )(core_row, normed, packed, packed_other)
    left_all = lax.all_to_all(
        left_t.reshape(8, rank // 8, rows), ("y", "core"), 0, 0, tiled=True
    )
    base = 8 * rank
    tail = jnp.stack(ordered(on_first, packed[:, base:], packed_other[:, base:]), 1)
    tail = tail.reshape(8, -1, rows).astype(jnp.float32)
    right_all = tail[:, :rank] + tail[:, rank : 2 * rank]
    ids_all = tail[:, 2 * rank].reshape(1, -1)
    right_flat = right_all.transpose(1, 0, 2).reshape(rank, -1)
    left_flat = left_all.transpose(1, 0, 2).reshape(8, 1, -1)
    doc_count = 64
    doc_range = jnp.arange(doc_count, dtype=jnp.float32)[:, None]
    onehot = (ids_all == doc_range).astype(jnp.float32)
    spread = (onehot[None] * left_flat).reshape(8 * doc_count, -1)
    doc_term = lax.dot_general(
        spread, right_flat, (((1,), (1,)), ((), ())), precision=lax.Precision.HIGHEST
    )
    doc_term, q_all = lax.optimization_barrier((doc_term, q_all))
    halves = after((y_ahead[:half], y_behind[half:]), doc_term)
    y_far = (from_y(halves[0], 1), from_y(halves[1], -1))
    doc_parts = lax.all_to_all(
        doc_term.reshape(64, 8, rank), ("zl", "zh", "x"), 0, 0, tiled=True
    )
    w_own = jnp.concatenate([w_z, y_ahead, y_behind, *after(y_far, doc_parts)], 0)
    w_other = swapped(w_own, "core")
    own_docs = jnp.sum(doc_parts, 0).astype(jnp.bfloat16)
    doc_low = spread_to_all(own_docs, DP)
    doc_low = doc_low.transpose(1, 0, 2).reshape(8, -1)
    scores = contract_last(doc_low, q_all)

    y_index, z_index = lax.axis_index("y"), lax.axis_index("zl")
    y_place = (y_index + jnp.array(Y_STEPS, jnp.int32)) % 4
    z_place = (z_index + jnp.array(Z_STEPS, jnp.int32)) % 8
    place = (y_place[:, None] * 8 + z_place[None, :]).reshape(32).astype(jnp.int32)
    values_out, hidden_grad = pl.pallas_call(
        layer_kernel,
        out_shape=(
            jax.ShapeDtypeStruct((rows, kv), jnp.bfloat16),
            jax.ShapeDtypeStruct((rows, width), jnp.bfloat16),
        ),
        in_specs=[smem, smem] + [vmem] * 7,
        out_specs=(vmem, vmem),
        compiler_params=params,
        name="layer",
    )(
        core_row, place, normed, hidden_in, norm_gain.reshape(1, width), inv_rms, value_grad,
        w_own, w_other,
    )
    return (values_out, hidden_grad, scores)


def solution(mesh):
    fine = Mesh(mesh.devices.reshape(4, 8, 2, 2, 4), DP + SCORE)
    tokens = SCORE + DP
    placed = (
        P(tokens, None),
        P(),
        P(DP, None),
        P(DP, None),
        P(tokens, None),
        P(),
        P(tokens),
        P(DP + SCORE, None),
    )
    return jax.shard_map(
        shards,
        mesh=fine,
        in_specs=placed,
        out_specs=(P(tokens, None), P(tokens, None), P(SCORE, DP)),
        check_vma=False,
    )
```

```python
import jax
import jax.numpy as jnp
from jax import lax
from jax.experimental import pallas as pl
from jax.experimental.pallas import tpu as pltpu
from jax.sharding import Mesh
from jax.sharding import PartitionSpec as P

EPSILON = 1e-05
DP = ("y", "zl", "core")
SCORE = ("zh", "x")
Y_STEPS = (0, 1, -1, 2)
Z_STEPS = (-1, 0, 1, 2, 3, 4, -3, -2)
BLOCK = 128
LIMIT = 24 * 1024 * 1024


def spread_to_all(value, axes):
    count = lax.axis_size(axes)
    copies = jnp.broadcast_to(value[None], (count,) + value.shape)
    return lax.all_to_all(copies, axes, 0, 0, tiled=True)


def swapped(value, axis):
    return lax.ppermute(value, axis, [(0, 1), (1, 0)])


def from_y(value, step):
    return lax.ppermute(value, "y", [((y + step) % 4, y) for y in range(4)])


def from_z(value, step):
    def place(z):
        return (z % 8) * 2 + z // 8

    return lax.ppermute(
        value, ("zl", "zh"), [(place((z + step) % 16), place(z)) for z in range(16)]
    )


def contract_last(left_side, right_side):
    return lax.dot_general(
        left_side, right_side, (((1,), (1,)), ((), ())), preferred_element_type=jnp.float32
    )


def ordered(first, own, other):
    return jnp.where(first, own, other), jnp.where(first, other, own)


def after(value, earlier):
    return lax.optimization_barrier((value, earlier))[0]


def left_kernel(core_ref, normed_ref, own_ref, other_ref, left_ref):
    first = core_ref[0] == 0
    rank = left_ref.shape[0]
    total = jnp.zeros(left_ref.shape, jnp.float32)
    for pair in range(32):
        y, z = divmod(pair, 8)
        own = own_ref[y, z * rank : (z + 1) * rank]
        other = other_ref[y, z * rank : (z + 1) * rank]
        factor = jnp.concatenate(ordered(first, own, other), 1)
        total += contract_last(factor, normed_ref[:, pair * 256 : (pair + 1) * 256])
    left_ref[...] = total


def joined_kernel(*refs):
    out_ref = refs[-1]
    start = 0
    for ref in refs[:-1]:
        out_ref[start : start + ref.shape[0]] = ref[...]
        start += ref.shape[0]


def halves_kernel(ahead_ref, behind_ref, low_ref, high_ref):
    half = low_ref.shape[0]
    low_ref[...] = ahead_ref[:half]
    high_ref[...] = behind_ref[half:]


def weights(first, own_ref, other_ref, pair):
    rows = slice(pair * BLOCK, (pair + 1) * BLOCK)
    return jnp.concatenate(ordered(first, own_ref[rows], other_ref[rows]), 0)


def columns(place_ref, pair):
    return pl.ds(pl.multiple_of(place_ref[pair] * 256, 256), 256)


def near_kernel(core_ref, place_ref, normed_ref, gain_ref, scale_ref, grad_ref, *refs):
    own_refs, other_refs, (total_ref, base_ref) = refs[:3], refs[3:6], refs[6:]
    first = core_ref[0] == 0
    grad = grad_ref[...]
    inv_rms = scale_ref[...]
    total = jnp.zeros(total_ref.shape, jnp.float32)
    for group in range(3):
        for step in range(8):
            pair = group * 8 + step
            where = columns(place_ref, pair)
            weight = weights(first, own_refs[group], other_refs[group], step)
            total += jnp.dot(normed_ref[:, where], weight, preferred_element_type=jnp.float32)
            back = contract_last(grad, weight) * gain_ref[:, where]
            base_ref[:, pair * 256 : (pair + 1) * 256] = inv_rms * back
    total_ref[...] = total


def far_kernel(
    core_ref, place_ref, normed_ref, hidden_ref, gain_ref, scale_ref, grad_ref, total_ref, base_ref,
    own_low, own_high, other_low, other_high, values_ref, hidden_grad_ref,
):
    first = core_ref[0] == 0
    width = normed_ref.shape[1]
    grad = grad_ref[...]
    inv_rms = scale_ref[...]
    own_refs, other_refs = (own_low, own_high), (other_low, other_high)
    total = total_ref[...]
    for step in range(8):
        weight = weights(first, own_refs[step // 4], other_refs[step // 4], step % 4)
        total += jnp.dot(
            normed_ref[:, columns(place_ref, 24 + step)], weight, preferred_element_type=jnp.float32
        )
    values_ref[...] = total.astype(jnp.bfloat16)
    along = jnp.sum(total * grad.astype(jnp.float32), axis=1, keepdims=True)
    pull = inv_rms * inv_rms * along / width
    for pair in range(32):
        where = columns(place_ref, pair)
        if pair < 24:
            base = base_ref[:, pair * 256 : (pair + 1) * 256]
        else:
            step = pair - 24
            weight = weights(first, own_refs[step // 4], other_refs[step // 4], step % 4)
            base = inv_rms * (contract_last(grad, weight) * gain_ref[:, where])
        wide = hidden_ref[:, where].astype(jnp.float32)
        hidden_grad_ref[:, where] = (base - wide * pull).astype(jnp.bfloat16)


def score_kernel(index_ref, docs_ref, here_ref, one_ref, two_ref, three_ref, scores_ref):
    lane = lax.broadcasted_iota(jnp.int32, docs_ref.shape[1:], 1)
    low = lane < docs_ref.shape[2] // 2
    pieces = []
    for pair in range(docs_ref.shape[0] // 2):
        even = docs_ref[2 * pair].astype(jnp.float32)
        odd = docs_ref[2 * pair + 1].astype(jnp.float32)
        pieces.append(jnp.where(low, even, odd).astype(jnp.bfloat16))
    docs = jnp.concatenate(pieces, 1)
    found = [contract_last(docs, ref[...]) for ref in (here_ref, one_ref, two_ref, three_ref)]
    size = here_ref.shape[0] // 2
    mine = [piece[:, :size] for piece in found]
    others = [piece[:, size:] for piece in found]
    zh, x = index_ref[0], index_ref[1]
    result = jnp.zeros(scores_ref.shape, jnp.float32)
    for turn in range(4):
        order = [(place - turn) % 4 for place in range(4)]
        one_half = [mine[step] for step in order]
        other_half = [others[step] for step in order]
        for side, parts in ((0, one_half + other_half), (1, other_half + one_half)):
            chosen = jnp.logical_and(zh == side, x == turn)
            result = jnp.where(chosen, jnp.concatenate(parts, 1), result)
    scores_ref[...] = result


def call(body, out_shape, scalars, name, limit=LIMIT):
    def run(*operands):
        smem = pl.BlockSpec(memory_space=pltpu.SMEM)
        vmem = pl.BlockSpec(memory_space=pltpu.VMEM)
        return pl.pallas_call(
            body,
            out_shape=out_shape,
            in_specs=[smem] * scalars + [vmem] * (len(operands) - scalars),
            out_specs=jax.tree.map(lambda _: vmem, out_shape),
            compiler_params=pltpu.CompilerParams(vmem_limit_bytes=limit),
            name=name,
        )(*operands)

    return run


def from_x(value, step):
    return lax.ppermute(value, "x", [((x + step) % 4, x) for x in range(4)])


def struct(shape, dtype):
    return jax.ShapeDtypeStruct(shape, dtype)


def shards(
    hidden_in, norm_gain, value_weight, input_proj, value_grad, output_proj, doc_ids, queries
):
    rows, width = hidden_in.shape
    kv = value_weight.shape[1]
    rank = input_proj.shape[1]
    core = lax.axis_index("core")
    core_row = core.astype(jnp.int32).reshape(1)
    on_first = core == 0

    factor = input_proj.T.reshape(4, 8, 2, BLOCK).transpose(0, 2, 1, 3).reshape(rank, BLOCK)
    right_t = lax.dot_general(
        output_proj, value_grad, (((0,), (1,)), ((), ())), preferred_element_type=jnp.float32
    ).astype(jnp.bfloat16)
    ids_rows = jnp.broadcast_to(doc_ids.astype(jnp.bfloat16)[None], (16, rows))
    factor_z = spread_to_all(factor, "zl").reshape(-1, BLOCK)
    packed = spread_to_all(jnp.concatenate([factor_z, right_t, ids_rows], 0), "y")
    packed_other = swapped(packed, "core")

    ahead, behind = from_z(value_weight, 1), from_z(value_weight, -1)
    three = call(joined_kernel, struct((3 * BLOCK, kv), jnp.bfloat16), 0, "near_three")
    two = call(joined_kernel, struct((2 * BLOCK, kv), jnp.bfloat16), 0, "near_two")
    near = after(three(behind, value_weight, ahead), factor_z)
    near_two = after(two(value_weight, ahead), factor_z)
    far_ahead, far_behind = from_z(near, 3), from_z(near_two, -3)

    wide_in = hidden_in.astype(jnp.float32)
    inv_rms = lax.rsqrt(jnp.mean(wide_in * wide_in, axis=1, keepdims=True) + EPSILON)
    normed = (wide_in * inv_rms * norm_gain).astype(jnp.bfloat16)
    left_t = call(left_kernel, struct((rank, rows), jnp.float32), 1, "left_factor")(
        core_row, normed, packed, packed_other
    )

    q_other = swapped(after(queries, left_t), "zh")

    left_all = lax.all_to_all(
        left_t.reshape(8, rank // 8, rows), ("y", "core"), 0, 0, tiled=True
    )

    far_ahead, far_behind = after((far_ahead, far_behind), left_all)
    w_z = call(joined_kernel, struct((8 * BLOCK, kv), jnp.bfloat16), 0, "along_z")(
        near, far_ahead, far_behind
    )
    y_ahead, y_behind = from_y(w_z, 1), from_y(w_z, -1)

    base = 8 * rank
    tail = jnp.stack(ordered(on_first, packed[:, base:], packed_other[:, base:]), 1)
    tail = tail.reshape(8, -1, rows).astype(jnp.float32)
    right_flat = tail[:, :rank].transpose(1, 0, 2).reshape(rank, -1)
    ids_all = tail[:, rank].reshape(1, -1)
    left_flat = left_all.transpose(1, 0, 2).reshape(8, 1, -1)
    doc_count = 64
    doc_range = jnp.arange(doc_count, dtype=jnp.float32)[:, None]
    onehot = (ids_all == doc_range).astype(jnp.float32)
    spread = (onehot[None] * left_flat).reshape(8 * doc_count, -1)
    doc_term = lax.dot_general(
        spread, right_flat, (((1,), (1,)), ((), ())), precision=lax.Precision.HIGHEST
    )
    doc_parts = lax.all_to_all(
        doc_term.reshape(64, 8, rank), ("zl", "zh", "x"), 0, 0, tiled=True
    )
    q_here = after(jnp.concatenate([queries, q_other], 0), doc_term)
    q_turns = [from_x(q_here, step) for step in (1, 2, 3)]
    w_z_other = swapped(w_z, "core")
    doc_parts, q_turns, w_z_other = lax.optimization_barrier((doc_parts, q_turns, w_z_other))
    own_docs = jnp.sum(doc_parts, 0).astype(jnp.bfloat16)
    own_docs = jnp.concatenate([own_docs, own_docs], 1)
    doc_copies = jnp.broadcast_to(own_docs[None], (64,) + own_docs.shape)
    y_ahead, y_behind, doc_copies = lax.optimization_barrier((y_ahead, y_behind, doc_copies))
    doc_low = lax.all_to_all(doc_copies, DP, 0, 0, tiled=True)
    low, high = call(
        halves_kernel, (struct((4 * BLOCK, kv), jnp.bfloat16),) * 2, 0, "far_halves"
    )(y_ahead, y_behind)
    y_low, y_high = from_y(low, 1), from_y(high, -1)

    y_index, z_index = lax.axis_index("y"), lax.axis_index("zl")
    y_place = (y_index + jnp.array(Y_STEPS, jnp.int32)) % 4
    z_place = (z_index + jnp.array(Z_STEPS, jnp.int32)) % 8
    place = (y_place[:, None] * 8 + z_place[None, :]).reshape(32).astype(jnp.int32)
    gain_row = norm_gain.reshape(1, width)
    total, near_base = call(
        near_kernel,
        (struct((rows, kv), jnp.float32), struct((rows, width * 3 // 4), jnp.float32)),
        2,
        "near_layer",
    )(
        core_row, place, normed, gain_row, inv_rms, value_grad, w_z, y_ahead, y_behind,
        w_z_other, swapped(y_ahead, "core"), swapped(y_behind, "core"),
    )
    doc_low, total = lax.optimization_barrier((doc_low, total))
    values_out, hidden_grad = call(
        far_kernel,
        (struct((rows, kv), jnp.bfloat16), struct((rows, width), jnp.bfloat16)),
        2,
        "far_layer",
    )(
        core_row, place, normed, hidden_in, gain_row, inv_rms, value_grad, total, near_base,
        y_low, y_high, swapped(y_low, "core"), swapped(y_high, "core"),
    )
    score_index = jnp.stack([lax.axis_index("zh"), lax.axis_index("x")]).astype(jnp.int32)
    scores = call(score_kernel, struct((8, 8 * queries.shape[0]), jnp.float32), 1, "scores")(
        score_index, doc_low, q_here, *q_turns
    )
    return (values_out, hidden_grad, scores)


def solution(mesh):
    fine = Mesh(mesh.devices.reshape(4, 8, 2, 2, 4), DP + SCORE)
    tokens = SCORE + DP
    placed = (
        P(tokens, None),
        P(),
        P(DP, None),
        P(DP, None),
        P(tokens, None),
        P(),
        P(tokens),
        P(DP + SCORE, None),
    )
    return jax.shard_map(
        shards,
        mesh=fine,
        in_specs=placed,
        out_specs=(P(tokens, None), P(tokens, None), P(SCORE, DP)),
        check_vma=False,
    )
```

```python
import jax
import jax.numpy as jnp
from jax import lax
from jax.experimental import pallas as pl
from jax.experimental.pallas import tpu as pltpu
from jax.sharding import Mesh
from jax.sharding import PartitionSpec as P

EPSILON = 1e-05
DP = ("y", "zl", "core")
SCORE = ("zh", "x")
BLOCK = 128
LIMIT = 32 * 1024 * 1024


def spread_to_all(value, axes):
    count = lax.axis_size(axes)
    copies = jnp.broadcast_to(value[None], (count,) + value.shape)
    return lax.all_to_all(copies, axes, 0, 0, tiled=True)


def swapped(value, axis):
    return lax.ppermute(value, axis, [(0, 1), (1, 0)])


def contract_last(left_side, right_side):
    return lax.dot_general(
        left_side, right_side, (((1,), (1,)), ((), ())), preferred_element_type=jnp.float32
    )


def ordered(first, own, other):
    return jnp.where(first, own, other), jnp.where(first, other, own)


def after(value, earlier):
    return lax.optimization_barrier((value, earlier))[0]


def left_kernel(core_ref, normed_ref, own_ref, other_ref, left_ref):
    first = core_ref[0] == 0
    rank = left_ref.shape[0]
    total = jnp.zeros(left_ref.shape, jnp.float32)
    for pair in range(32):
        y, z = divmod(pair, 8)
        own = own_ref[y, z * rank : (z + 1) * rank]
        other = other_ref[y, z * rank : (z + 1) * rank]
        factor = jnp.concatenate(ordered(first, own, other), 1)
        total += contract_last(factor, normed_ref[:, pair * 256 : (pair + 1) * 256])
    left_ref[...] = total


def layer_kernel(
    normed_ref, hidden_ref, gain_ref, scale_ref, grad_ref, weight_ref,
    values_ref, hidden_grad_ref, held, base, wide_in, arrived,
):
    chunks = held.shape[0]
    depth = held.shape[1]
    width = normed_ref.shape[1]
    copies = [
        pltpu.make_async_copy(
            weight_ref.at[pl.ds(chunk * depth, depth)], held.at[chunk], arrived.at[chunk]
        )
        for chunk in range(chunks)
    ]
    for copy in copies:
        copy.start()
    hidden_copy = pltpu.make_async_copy(hidden_ref, wide_in, arrived.at[chunks])
    hidden_copy.start()
    grad = grad_ref[...]
    inv_rms = scale_ref[...]
    total = jnp.zeros(values_ref.shape, jnp.float32)
    for chunk, copy in enumerate(copies):
        copy.wait()
        for start in range(0, depth, 256):
            where = slice(chunk * depth + start, chunk * depth + start + 256)
            weight = held[chunk, start : start + 256]
            total += jnp.dot(normed_ref[:, where], weight, preferred_element_type=jnp.float32)
            base[:, where] = inv_rms * (contract_last(grad, weight) * gain_ref[:, where])
    values_ref[...] = total.astype(jnp.bfloat16)
    along = jnp.sum(total * grad.astype(jnp.float32), axis=1, keepdims=True)
    pull = inv_rms * inv_rms * along / width
    hidden_copy.wait()
    for start in range(0, width, 512):
        where = slice(start, start + 512)
        wide = wide_in[:, where].astype(jnp.float32)
        hidden_grad_ref[:, where] = (base[:, where] - wide * pull).astype(jnp.bfloat16)


def score_kernel(index_ref, docs_ref, here_ref, one_ref, two_ref, three_ref, scores_ref):
    lane = lax.broadcasted_iota(jnp.int32, docs_ref.shape[1:], 1)
    low = lane < docs_ref.shape[2] // 2
    pieces = []
    for pair in range(docs_ref.shape[0] // 2):
        even = docs_ref[2 * pair].astype(jnp.float32)
        odd = docs_ref[2 * pair + 1].astype(jnp.float32)
        pieces.append(jnp.where(low, even, odd).astype(jnp.bfloat16))
    docs = jnp.concatenate(pieces, 1)
    found = [contract_last(docs, ref[...]) for ref in (here_ref, one_ref, two_ref, three_ref)]
    size = here_ref.shape[0] // 2
    mine = [piece[:, :size] for piece in found]
    others = [piece[:, size:] for piece in found]
    zh, x = index_ref[0], index_ref[1]
    result = jnp.zeros(scores_ref.shape, jnp.float32)
    for turn in range(4):
        order = [(place - turn) % 4 for place in range(4)]
        one_half = [mine[step] for step in order]
        other_half = [others[step] for step in order]
        for side, parts in ((0, one_half + other_half), (1, other_half + one_half)):
            chosen = jnp.logical_and(zh == side, x == turn)
            result = jnp.where(chosen, jnp.concatenate(parts, 1), result)
    scores_ref[...] = result


def call(body, out_shape, scalars, name, limit=LIMIT):
    def run(*operands):
        smem = pl.BlockSpec(memory_space=pltpu.SMEM)
        vmem = pl.BlockSpec(memory_space=pltpu.VMEM)
        return pl.pallas_call(
            body,
            out_shape=out_shape,
            in_specs=[smem] * scalars + [vmem] * (len(operands) - scalars),
            out_specs=jax.tree.map(lambda _: vmem, out_shape),
            compiler_params=pltpu.CompilerParams(vmem_limit_bytes=limit),
            name=name,
        )(*operands)

    return run


def from_x(value, step):
    return lax.ppermute(value, "x", [((x + step) % 4, x) for x in range(4)])


def struct(shape, dtype):
    return jax.ShapeDtypeStruct(shape, dtype)


def shards(
    hidden_in, norm_gain, value_weight, input_proj, value_grad, output_proj, doc_ids, queries
):
    rows, width = hidden_in.shape
    kv = value_weight.shape[1]
    rank = input_proj.shape[1]
    core = lax.axis_index("core")
    core_row = core.astype(jnp.int32).reshape(1)
    on_first = core == 0

    factor = input_proj.T.reshape(4, 8, 2, BLOCK).transpose(0, 2, 1, 3).reshape(rank, BLOCK)
    right_t = lax.dot_general(
        output_proj, value_grad, (((0,), (1,)), ((), ())), preferred_element_type=jnp.float32
    ).astype(jnp.bfloat16)
    ids_rows = jnp.broadcast_to(doc_ids.astype(jnp.bfloat16)[None], (16, rows))
    factor_z = spread_to_all(factor, "zl").reshape(-1, BLOCK)
    packed = spread_to_all(jnp.concatenate([factor_z, right_t, ids_rows], 0), "y")
    packed_other = swapped(packed, "core")

    w_all = lax.all_gather(value_weight, DP, axis=0, tiled=True)

    wide_in = hidden_in.astype(jnp.float32)
    inv_rms = lax.rsqrt(jnp.mean(wide_in * wide_in, axis=1, keepdims=True) + EPSILON)
    normed = (wide_in * inv_rms * norm_gain).astype(jnp.bfloat16)
    left_t = call(left_kernel, struct((rank, rows), jnp.float32), 1, "left_factor")(
        core_row, normed, packed, packed_other
    )

    q_other = swapped(after(queries, left_t), "zh")

    left_all = lax.all_to_all(
        left_t.reshape(8, rank // 8, rows), ("y", "core"), 0, 0, tiled=True
    )

    base = 8 * rank
    tail = jnp.stack(ordered(on_first, packed[:, base:], packed_other[:, base:]), 1)
    tail = tail.reshape(8, -1, rows).astype(jnp.float32)
    right_flat = tail[:, :rank].transpose(1, 0, 2).reshape(rank, -1)
    ids_all = tail[:, rank].reshape(1, -1)
    left_flat = left_all.transpose(1, 0, 2).reshape(8, 1, -1)
    doc_count = 64
    doc_range = jnp.arange(doc_count, dtype=jnp.float32)[:, None]
    onehot = (ids_all == doc_range).astype(jnp.float32)
    spread = (onehot[None] * left_flat).reshape(8 * doc_count, -1)
    doc_term = lax.dot_general(
        spread, right_flat, (((1,), (1,)), ((), ())), precision=lax.Precision.HIGHEST
    )
    doc_parts = lax.all_to_all(
        doc_term.reshape(64, 8, rank), ("zl", "zh", "x"), 0, 0, tiled=True
    )
    q_here = after(jnp.concatenate([queries, q_other], 0), doc_term)
    q_turns = [from_x(q_here, step) for step in (1, 2, 3)]
    doc_parts, q_turns = lax.optimization_barrier((doc_parts, q_turns))
    own_docs = jnp.sum(doc_parts, 0).astype(jnp.bfloat16)
    doc_low = spread_to_all(jnp.concatenate([own_docs, own_docs], 1), DP)

    vmem = pl.BlockSpec(memory_space=pltpu.VMEM)
    hbm = pl.BlockSpec(memory_space=pltpu.HBM)
    chunks = 8
    values_out, hidden_grad = pl.pallas_call(
        layer_kernel,
        out_shape=(struct((rows, kv), jnp.bfloat16), struct((rows, width), jnp.bfloat16)),
        in_specs=[vmem, hbm, vmem, vmem, vmem, hbm],
        out_specs=(vmem, vmem),
        scratch_shapes=[
            pltpu.VMEM((chunks, width // chunks, kv), jnp.bfloat16),
            pltpu.VMEM((rows, width), jnp.float32),
            pltpu.VMEM((rows, width), jnp.bfloat16),
            pltpu.SemaphoreType.DMA((chunks + 1,)),
        ],
        compiler_params=pltpu.CompilerParams(vmem_limit_bytes=LIMIT),
        name="layer",
    )(normed, hidden_in, norm_gain.reshape(1, width), inv_rms, value_grad, w_all)
    score_index = jnp.stack([lax.axis_index("zh"), lax.axis_index("x")]).astype(jnp.int32)
    scores = call(score_kernel, struct((8, 8 * queries.shape[0]), jnp.float32), 1, "scores")(
        score_index, doc_low, q_here, *q_turns
    )
    return (values_out, hidden_grad, scores)


def solution(mesh):
    fine = Mesh(mesh.devices.reshape(4, 8, 2, 2, 4), DP + SCORE)
    tokens = SCORE + DP
    placed = (
        P(tokens, None),
        P(),
        P(DP, None),
        P(DP, None),
        P(tokens, None),
        P(),
        P(tokens),
        P(DP + SCORE, None),
    )
    return jax.shard_map(
        shards,
        mesh=fine,
        in_specs=placed,
        out_specs=(P(tokens, None), P(tokens, None), P(SCORE, DP)),
        check_vma=False,
    )
```

```python
import jax
import jax.numpy as jnp
from jax import lax
from jax.experimental import pallas as pl
from jax.experimental.pallas import tpu as pltpu
from jax.sharding import Mesh
from jax.sharding import PartitionSpec as P

EPSILON = 1e-05
DP = ("y", "zl", "core")
SCORE = ("zh", "x")
Z_STEPS = (-1, 0, 1, 2, 3, 4, -3, -2)
BLOCK = 128
LIMIT = 16 * 1024 * 1024


def spread_to_all(value, axes):
    count = lax.axis_size(axes)
    copies = jnp.broadcast_to(value[None], (count,) + value.shape)
    return lax.all_to_all(copies, axes, 0, 0, tiled=True)


def swapped(value, axis):
    return lax.ppermute(value, axis, [(0, 1), (1, 0)])


def from_z(value, step):
    def place(z):
        return (z % 8) * 2 + z // 8

    return lax.ppermute(
        value, ("zl", "zh"), [(place((z + step) % 16), place(z)) for z in range(16)]
    )


def contract_last(left_side, right_side):
    return lax.dot_general(
        left_side, right_side, (((1,), (1,)), ((), ())), preferred_element_type=jnp.float32
    )


def ordered(first, own, other):
    return jnp.where(first, own, other), jnp.where(first, other, own)


def after(value, earlier):
    return lax.optimization_barrier((value, earlier))[0]


def left_kernel(core_ref, normed_ref, own_ref, other_ref, left_ref):
    first = core_ref[0] == 0
    rank = left_ref.shape[0]
    total = jnp.zeros(left_ref.shape, jnp.float32)
    for pair in range(32):
        y, z = divmod(pair, 8)
        own = own_ref[y, z * rank : (z + 1) * rank]
        other = other_ref[y, z * rank : (z + 1) * rank]
        factor = jnp.concatenate(ordered(first, own, other), 1)
        total += contract_last(factor, normed_ref[:, pair * 256 : (pair + 1) * 256])
    left_ref[...] = total


def joined_kernel(*refs):
    out_ref = refs[-1]
    start = 0
    for ref in refs[:-1]:
        out_ref[start : start + ref.shape[0]] = ref[...]
        start += ref.shape[0]


def along_z_kernel(near_ref, ahead_ref, behind_ref, out_ref):
    three = 3 * BLOCK
    out_ref[:three] = near_ref[...]
    out_ref[three : 2 * three] = ahead_ref[...]
    out_ref[2 * three :] = behind_ref[BLOCK:]


def layer_kernel(
    place_ref, normed_hbm, hidden_hbm, gain_ref, scale_ref, grad_ref, weight_hbm,
    values_ref, hidden_grad_ref, held, base, normed_ref, hidden_ref, arrived,
):
    chunks, depth = held.shape[:2]
    width = normed_ref.shape[1]
    copies = [
        pltpu.make_async_copy(
            weight_hbm.at[pl.ds(chunk * depth, depth)], held.at[chunk], arrived.at[chunk]
        )
        for chunk in range(chunks)
    ]
    normed_copy = pltpu.make_async_copy(normed_hbm, normed_ref, arrived.at[chunks])
    hidden_copy = pltpu.make_async_copy(hidden_hbm, hidden_ref, arrived.at[chunks + 1])
    normed_copy.start()
    for copy in copies:
        copy.start()
    hidden_copy.start()
    grad = grad_ref[...]
    inv_rms = scale_ref[...]
    total = jnp.zeros(values_ref.shape, jnp.float32)
    normed_copy.wait()
    for y in range(chunks // 2):
        copies[2 * y].wait()
        copies[2 * y + 1].wait()
        for step in range(depth // BLOCK):
            rows = slice(step * BLOCK, (step + 1) * BLOCK)
            weight = jnp.concatenate([held[2 * y, rows], held[2 * y + 1, rows]], 0)
            offset = pl.multiple_of(y * (width // 4) + place_ref[step] * 256, 256)
            where = pl.ds(offset, 256)
            total += jnp.dot(normed_ref[:, where], weight, preferred_element_type=jnp.float32)
            base[:, where] = inv_rms * (contract_last(grad, weight) * gain_ref[:, where])
    values_ref[...] = total.astype(jnp.bfloat16)
    along = jnp.sum(total * grad.astype(jnp.float32), axis=1, keepdims=True)
    pull = inv_rms * inv_rms * along / width
    hidden_copy.wait()
    for start in range(0, width, 512):
        where = slice(start, start + 512)
        wide = hidden_ref[:, where].astype(jnp.float32)
        hidden_grad_ref[:, where] = (base[:, where] - wide * pull).astype(jnp.bfloat16)


def score_kernel(index_ref, docs_ref, here_ref, one_ref, two_ref, three_ref, scores_ref):
    lane = lax.broadcasted_iota(jnp.int32, docs_ref.shape[1:], 1)
    low = lane < docs_ref.shape[2] // 2
    pieces = []
    for pair in range(docs_ref.shape[0] // 2):
        even = docs_ref[2 * pair].astype(jnp.float32)
        odd = docs_ref[2 * pair + 1].astype(jnp.float32)
        pieces.append(jnp.where(low, even, odd).astype(jnp.bfloat16))
    docs = jnp.concatenate(pieces, 1)
    found = [contract_last(docs, ref[...]) for ref in (here_ref, one_ref, two_ref, three_ref)]
    size = here_ref.shape[0] // 2
    mine = [piece[:, :size] for piece in found]
    others = [piece[:, size:] for piece in found]
    zh, x = index_ref[0], index_ref[1]
    result = jnp.zeros(scores_ref.shape, jnp.float32)
    for turn in range(4):
        order = [(place - turn) % 4 for place in range(4)]
        one_half = [mine[step] for step in order]
        other_half = [others[step] for step in order]
        for side, parts in ((0, one_half + other_half), (1, other_half + one_half)):
            chosen = jnp.logical_and(zh == side, x == turn)
            result = jnp.where(chosen, jnp.concatenate(parts, 1), result)
    scores_ref[...] = result


def call(body, out_shape, scalars, name, limit=LIMIT):
    def run(*operands):
        smem = pl.BlockSpec(memory_space=pltpu.SMEM)
        vmem = pl.BlockSpec(memory_space=pltpu.VMEM)
        return pl.pallas_call(
            body,
            out_shape=out_shape,
            in_specs=[smem] * scalars + [vmem] * (len(operands) - scalars),
            out_specs=jax.tree.map(lambda _: vmem, out_shape),
            compiler_params=pltpu.CompilerParams(vmem_limit_bytes=limit),
            name=name,
        )(*operands)

    return run


def from_x(value, step):
    return lax.ppermute(value, "x", [((x + step) % 4, x) for x in range(4)])


def struct(shape, dtype):
    return jax.ShapeDtypeStruct(shape, dtype)


def shards(
    hidden_in, norm_gain, value_weight, input_proj, value_grad, output_proj, doc_ids, queries
):
    rows, width = hidden_in.shape
    kv = value_weight.shape[1]
    rank = input_proj.shape[1]
    core = lax.axis_index("core")
    core_row = core.astype(jnp.int32).reshape(1)
    on_first = core == 0

    factor = input_proj.T.reshape(4, 8, 2, BLOCK).transpose(0, 2, 1, 3).reshape(rank, BLOCK)
    right_t = lax.dot_general(
        output_proj, value_grad, (((0,), (1,)), ((), ())), preferred_element_type=jnp.float32
    ).astype(jnp.bfloat16)
    ids_rows = jnp.broadcast_to(doc_ids.astype(jnp.bfloat16)[None], (16, rows))
    factor_z = spread_to_all(factor, "zl").reshape(-1, BLOCK)
    packed = spread_to_all(jnp.concatenate([factor_z, right_t, ids_rows], 0), "y")
    packed_other = swapped(packed, "core")

    ahead, behind = from_z(value_weight, 1), from_z(value_weight, -1)
    near = call(joined_kernel, struct((3 * BLOCK, kv), jnp.bfloat16), 0, "near_three")(
        behind, value_weight, ahead
    )
    near = after(near, factor_z)
    far_ahead, far_behind = from_z(near, 3), from_z(near, -3)

    wide_in = hidden_in.astype(jnp.float32)
    inv_rms = lax.rsqrt(jnp.mean(wide_in * wide_in, axis=1, keepdims=True) + EPSILON)
    normed = (wide_in * inv_rms * norm_gain).astype(jnp.bfloat16)
    left_t = call(left_kernel, struct((rank, rows), jnp.float32), 1, "left_factor")(
        core_row, normed, packed, packed_other
    )

    w_z = call(along_z_kernel, struct((8 * BLOCK, kv), jnp.bfloat16), 0, "along_z")(
        near, *after((far_ahead, far_behind), left_t)
    )
    w_all = lax.all_gather(w_z, ("y", "core"), axis=0, tiled=True)
    z_place = (lax.axis_index("zl") + jnp.array(Z_STEPS, jnp.int32)) % 8

    q_other = swapped(after(queries, left_t), "zh")

    left_all = lax.all_to_all(
        left_t.reshape(8, rank // 8, rows), ("y", "core"), 0, 0, tiled=True
    )

    base = 8 * rank
    tail = jnp.stack(ordered(on_first, packed[:, base:], packed_other[:, base:]), 1)
    tail = tail.reshape(8, -1, rows).astype(jnp.float32)
    right_flat = tail[:, :rank].transpose(1, 0, 2).reshape(rank, -1)
    ids_all = tail[:, rank].reshape(1, -1)
    left_flat = left_all.transpose(1, 0, 2).reshape(8, 1, -1)
    doc_count = 64
    doc_range = jnp.arange(doc_count, dtype=jnp.float32)[:, None]
    onehot = (ids_all == doc_range).astype(jnp.float32)
    spread = (onehot[None] * left_flat).reshape(8 * doc_count, -1)
    doc_term = lax.dot_general(
        spread, right_flat, (((1,), (1,)), ((), ())), precision=lax.Precision.HIGHEST
    )
    doc_parts = lax.all_to_all(
        doc_term.reshape(64, 8, rank), ("zl", "zh", "x"), 0, 0, tiled=True
    )
    q_here = after(jnp.concatenate([queries, q_other], 0), doc_term)
    q_turns = [from_x(q_here, step) for step in (1, 2, 3)]
    own_docs = jnp.sum(doc_parts, 0).astype(jnp.bfloat16)
    doc_low = spread_to_all(jnp.concatenate([own_docs, own_docs], 1), DP)

    vmem = pl.BlockSpec(memory_space=pltpu.VMEM)
    hbm = pl.BlockSpec(memory_space=pltpu.HBM)
    chunks = 8
    values_out, hidden_grad = pl.pallas_call(
        layer_kernel,
        out_shape=(struct((rows, kv), jnp.bfloat16), struct((rows, width), jnp.bfloat16)),
        in_specs=[pl.BlockSpec(memory_space=pltpu.SMEM), hbm, hbm, vmem, vmem, vmem, hbm],
        out_specs=(vmem, vmem),
        scratch_shapes=[
            pltpu.VMEM((chunks, width // chunks, kv), jnp.bfloat16),
            pltpu.VMEM((rows, width), jnp.float32),
            pltpu.VMEM((rows, width), jnp.bfloat16),
            pltpu.VMEM((rows, width), jnp.bfloat16),
            pltpu.SemaphoreType.DMA((chunks + 2,)),
        ],
        compiler_params=pltpu.CompilerParams(vmem_limit_bytes=58 * 1024 * 1024),
        name="layer",
    )(
        z_place.astype(jnp.int32), normed, hidden_in, norm_gain.reshape(1, width), inv_rms,
        value_grad, w_all,
    )
    doc_low, values_out = lax.optimization_barrier((doc_low, values_out))
    score_index = jnp.stack([lax.axis_index("zh"), lax.axis_index("x")]).astype(jnp.int32)
    scores = call(score_kernel, struct((8, 8 * queries.shape[0]), jnp.float32), 1, "scores")(
        score_index, doc_low, q_here, *q_turns
    )
    return (values_out, hidden_grad, scores)


def solution(mesh):
    fine = Mesh(mesh.devices.reshape(4, 8, 2, 2, 4), DP + SCORE)
    tokens = SCORE + DP
    placed = (
        P(tokens, None),
        P(),
        P(DP, None),
        P(DP, None),
        P(tokens, None),
        P(),
        P(tokens),
        P(DP + SCORE, None),
    )
    return jax.shard_map(
        shards,
        mesh=fine,
        in_specs=placed,
        out_specs=(P(tokens, None), P(tokens, None), P(SCORE, DP)),
        check_vma=False,
    )
```

```python
import jax
import jax.numpy as jnp
from jax import lax
from jax.experimental import pallas as pl
from jax.experimental.pallas import tpu as pltpu
from jax.sharding import Mesh
from jax.sharding import PartitionSpec as P

EPSILON = 1e-05
DP = ("y", "zl", "core")
SCORE = ("zh", "x")
Z_STEPS = (-1, 0, 1, 2, 3, 4, -3, -2)
BLOCK = 128
LIMIT = 16 * 1024 * 1024


def spread_to_all(value, axes):
    count = lax.axis_size(axes)
    copies = jnp.broadcast_to(value[None], (count,) + value.shape)
    return lax.all_to_all(copies, axes, 0, 0, tiled=True)


def swapped(value, axis):
    return lax.ppermute(value, axis, [(0, 1), (1, 0)])


def from_z(value, step):
    def place(z):
        return (z % 8) * 2 + z // 8

    return lax.ppermute(
        value, ("zl", "zh"), [(place((z + step) % 16), place(z)) for z in range(16)]
    )


def contract_last(left_side, right_side):
    return lax.dot_general(
        left_side, right_side, (((1,), (1,)), ((), ())), preferred_element_type=jnp.float32
    )


def ordered(first, own, other):
    return jnp.where(first, own, other), jnp.where(first, other, own)


def after(value, earlier):
    return lax.optimization_barrier((value, earlier))[0]


def left_kernel(core_ref, normed_ref, own_ref, other_ref, left_ref):
    first = core_ref[0] == 0
    rank = left_ref.shape[0]
    total = jnp.zeros(left_ref.shape, jnp.float32)
    for pair in range(32):
        y, z = divmod(pair, 8)
        own = own_ref[y, z * rank : (z + 1) * rank]
        other = other_ref[y, z * rank : (z + 1) * rank]
        factor = jnp.concatenate(ordered(first, own, other), 1)
        total += contract_last(factor, normed_ref[:, pair * 256 : (pair + 1) * 256])
    left_ref[...] = total


def joined_kernel(*refs):
    out_ref = refs[-1]
    start = 0
    for ref in refs[:-1]:
        out_ref[start : start + ref.shape[0]] = ref[...]
        start += ref.shape[0]


def along_z_kernel(near_ref, ahead_ref, behind_ref, out_ref):
    three = 3 * BLOCK
    out_ref[:three] = near_ref[...]
    out_ref[three : 2 * three] = ahead_ref[...]
    out_ref[2 * three :] = behind_ref[BLOCK:]


def layer_kernel(
    place_ref, normed_hbm, hidden_hbm, gain_ref, scale_ref, grad_ref, weight_hbm,
    values_ref, hidden_grad_ref, held, base, normed_ref, hidden_ref, arrived,
):
    chunks, depth = held.shape[:2]
    width = normed_ref.shape[1]
    copies = [
        pltpu.make_async_copy(
            weight_hbm.at[pl.ds((chunk * 4 + part) * depth, depth)],
            held.at[chunk, :, pl.ds(part * BLOCK, BLOCK)],
            arrived.at[chunk * 4 + part],
        )
        for chunk in range(chunks)
        for part in range(4)
    ]
    normed_copy = pltpu.make_async_copy(normed_hbm, normed_ref, arrived.at[4 * chunks])
    hidden_copy = pltpu.make_async_copy(hidden_hbm, hidden_ref, arrived.at[4 * chunks + 1])
    normed_copy.start()
    for copy in copies:
        copy.start()
    hidden_copy.start()
    grad = grad_ref[...]
    inv_rms = scale_ref[...]
    total = jnp.zeros(values_ref.shape, jnp.float32)
    normed_copy.wait()
    for y in range(chunks // 2):
        for copy in copies[8 * y : 8 * y + 8]:
            copy.wait()
        for step in range(depth // BLOCK):
            rows = slice(step * BLOCK, (step + 1) * BLOCK)
            weight = jnp.concatenate([held[2 * y, rows], held[2 * y + 1, rows]], 0)
            offset = pl.multiple_of(y * (width // 4) + place_ref[step] * 256, 256)
            where = pl.ds(offset, 256)
            total += jnp.dot(normed_ref[:, where], weight, preferred_element_type=jnp.float32)
            base[:, where] = inv_rms * (contract_last(grad, weight) * gain_ref[:, where])
    values_ref[...] = total.astype(jnp.bfloat16)
    along = jnp.sum(total * grad.astype(jnp.float32), axis=1, keepdims=True)
    pull = inv_rms * inv_rms * along / width
    hidden_copy.wait()
    for start in range(0, width, 512):
        where = slice(start, start + 512)
        wide = hidden_ref[:, where].astype(jnp.float32)
        hidden_grad_ref[:, where] = (base[:, where] - wide * pull).astype(jnp.bfloat16)


def score_kernel(index_ref, docs_ref, here_ref, one_ref, two_ref, three_ref, scores_ref):
    lane = lax.broadcasted_iota(jnp.int32, docs_ref.shape[1:], 1)
    low = lane < docs_ref.shape[2] // 2
    pieces = []
    for pair in range(docs_ref.shape[0] // 2):
        even = docs_ref[2 * pair].astype(jnp.float32)
        odd = docs_ref[2 * pair + 1].astype(jnp.float32)
        pieces.append(jnp.where(low, even, odd).astype(jnp.bfloat16))
    docs = jnp.concatenate(pieces, 1)
    found = [contract_last(docs, ref[...]) for ref in (here_ref, one_ref, two_ref, three_ref)]
    size = here_ref.shape[0] // 2
    mine = [piece[:, :size] for piece in found]
    others = [piece[:, size:] for piece in found]
    zh, x = index_ref[0], index_ref[1]
    result = jnp.zeros(scores_ref.shape, jnp.float32)
    for turn in range(4):
        order = [(place - turn) % 4 for place in range(4)]
        one_half = [mine[step] for step in order]
        other_half = [others[step] for step in order]
        for side, parts in ((0, one_half + other_half), (1, other_half + one_half)):
            chosen = jnp.logical_and(zh == side, x == turn)
            result = jnp.where(chosen, jnp.concatenate(parts, 1), result)
    scores_ref[...] = result


def call(body, out_shape, scalars, name, limit=LIMIT):
    def run(*operands):
        smem = pl.BlockSpec(memory_space=pltpu.SMEM)
        vmem = pl.BlockSpec(memory_space=pltpu.VMEM)
        return pl.pallas_call(
            body,
            out_shape=out_shape,
            in_specs=[smem] * scalars + [vmem] * (len(operands) - scalars),
            out_specs=jax.tree.map(lambda _: vmem, out_shape),
            compiler_params=pltpu.CompilerParams(vmem_limit_bytes=limit),
            name=name,
        )(*operands)

    return run


def from_x(value, step):
    return lax.ppermute(value, "x", [((x + step) % 4, x) for x in range(4)])


def struct(shape, dtype):
    return jax.ShapeDtypeStruct(shape, dtype)


def shards(
    hidden_in, norm_gain, value_weight, input_proj, value_grad, output_proj, doc_ids, queries
):
    rows, width = hidden_in.shape
    kv = value_weight.shape[1]
    rank = input_proj.shape[1]
    core = lax.axis_index("core")
    core_row = core.astype(jnp.int32).reshape(1)
    on_first = core == 0

    factor = input_proj.T.reshape(4, 8, 2, BLOCK).transpose(0, 2, 1, 3).reshape(rank, BLOCK)
    right_t = lax.dot_general(
        output_proj, value_grad, (((0,), (1,)), ((), ())), preferred_element_type=jnp.float32
    ).astype(jnp.bfloat16)
    ids_rows = jnp.broadcast_to(doc_ids.astype(jnp.bfloat16)[None], (16, rows))
    factor_z = spread_to_all(factor, "zl").reshape(-1, BLOCK)
    packed = spread_to_all(jnp.concatenate([factor_z, right_t, ids_rows], 0), "y")
    packed_other = swapped(packed, "core")

    quarter = lax.dynamic_slice_in_dim(value_weight, lax.axis_index("x") * BLOCK, BLOCK, 1)
    ahead, behind = from_z(quarter, 1), from_z(quarter, -1)
    near = call(joined_kernel, struct((3 * BLOCK, BLOCK), jnp.bfloat16), 0, "near_three")(
        behind, quarter, ahead
    )
    near = after(near, factor_z)
    far_ahead, far_behind = from_z(near, 3), from_z(near, -3)

    wide_in = hidden_in.astype(jnp.float32)
    inv_rms = lax.rsqrt(jnp.mean(wide_in * wide_in, axis=1, keepdims=True) + EPSILON)
    normed = (wide_in * inv_rms * norm_gain).astype(jnp.bfloat16)
    left_t = call(left_kernel, struct((rank, rows), jnp.float32), 1, "left_factor")(
        core_row, normed, packed, packed_other
    )

    w_z = call(along_z_kernel, struct((8 * BLOCK, BLOCK), jnp.bfloat16), 0, "along_z")(
        near, *after((far_ahead, far_behind), left_t)
    )
    w_all = lax.all_gather(w_z, ("y", "core", "x"), axis=0, tiled=True)
    z_place = (lax.axis_index("zl") + jnp.array(Z_STEPS, jnp.int32)) % 8

    q_other = swapped(after(queries, left_t), "zh")

    left_all = lax.all_to_all(
        left_t.reshape(8, rank // 8, rows), ("y", "core"), 0, 0, tiled=True
    )

    base = 8 * rank
    tail = jnp.stack(ordered(on_first, packed[:, base:], packed_other[:, base:]), 1)
    tail = tail.reshape(8, -1, rows).astype(jnp.float32)
    right_flat = tail[:, :rank].transpose(1, 0, 2).reshape(rank, -1)
    ids_all = tail[:, rank].reshape(1, -1)
    left_flat = left_all.transpose(1, 0, 2).reshape(8, 1, -1)
    doc_count = 64
    doc_range = jnp.arange(doc_count, dtype=jnp.float32)[:, None]
    onehot = (ids_all == doc_range).astype(jnp.float32)
    spread = (onehot[None] * left_flat).reshape(8 * doc_count, -1)
    doc_term = lax.dot_general(
        spread, right_flat, (((1,), (1,)), ((), ())), precision=lax.Precision.HIGHEST
    )
    doc_parts = lax.all_to_all(
        doc_term.reshape(64, 8, rank), ("zl", "zh", "x"), 0, 0, tiled=True
    )
    q_here = after(jnp.concatenate([queries, q_other], 0), doc_term)
    q_turns = [from_x(q_here, step) for step in (1, 2, 3)]
    own_docs = jnp.sum(doc_parts, 0).astype(jnp.bfloat16)
    doc_low = spread_to_all(jnp.concatenate([own_docs, own_docs], 1), DP)

    vmem = pl.BlockSpec(memory_space=pltpu.VMEM)
    hbm = pl.BlockSpec(memory_space=pltpu.HBM)
    chunks = 8
    values_out, hidden_grad = pl.pallas_call(
        layer_kernel,
        out_shape=(struct((rows, kv), jnp.bfloat16), struct((rows, width), jnp.bfloat16)),
        in_specs=[pl.BlockSpec(memory_space=pltpu.SMEM), hbm, hbm, vmem, vmem, vmem, hbm],
        out_specs=(vmem, vmem),
        scratch_shapes=[
            pltpu.VMEM((chunks, width // chunks, kv), jnp.bfloat16),
            pltpu.VMEM((rows, width), jnp.float32),
            pltpu.VMEM((rows, width), jnp.bfloat16),
            pltpu.VMEM((rows, width), jnp.bfloat16),
            pltpu.SemaphoreType.DMA((4 * chunks + 2,)),
        ],
        compiler_params=pltpu.CompilerParams(vmem_limit_bytes=58 * 1024 * 1024),
        name="layer",
    )(
        z_place.astype(jnp.int32), normed, hidden_in, norm_gain.reshape(1, width), inv_rms,
        value_grad, w_all,
    )
    doc_low, values_out = lax.optimization_barrier((doc_low, values_out))
    score_index = jnp.stack([lax.axis_index("zh"), lax.axis_index("x")]).astype(jnp.int32)
    scores = call(score_kernel, struct((8, 8 * queries.shape[0]), jnp.float32), 1, "scores")(
        score_index, doc_low, q_here, *q_turns
    )
    return (values_out, hidden_grad, scores)


def solution(mesh):
    fine = Mesh(mesh.devices.reshape(4, 8, 2, 2, 4), DP + SCORE)
    tokens = SCORE + DP
    placed = (
        P(tokens, None),
        P(),
        P(DP, None),
        P(DP, None),
        P(tokens, None),
        P(),
        P(tokens),
        P(DP + SCORE, None),
    )
    return jax.shard_map(
        shards,
        mesh=fine,
        in_specs=placed,
        out_specs=(P(tokens, None), P(tokens, None), P(SCORE, DP)),
        check_vma=False,
    )
```

```python
import jax
import jax.numpy as jnp
from jax import lax
from jax.experimental import pallas as pl
from jax.experimental.pallas import tpu as pltpu
from jax.sharding import Mesh
from jax.sharding import PartitionSpec as P

EPSILON = 1e-05
DP = ("y", "zl", "core")
SCORE = ("zh", "x")
Z_STEPS = (-1, 0, 1, 2, 3, 4, -3, -2)
BLOCK = 128
LIMIT = 16 * 1024 * 1024


def spread_to_all(value, axes):
    count = lax.axis_size(axes)
    copies = jnp.broadcast_to(value[None], (count,) + value.shape)
    return lax.all_to_all(copies, axes, 0, 0, tiled=True)


def swapped(value, axis):
    return lax.ppermute(value, axis, [(0, 1), (1, 0)])


def from_z(value, step):
    def place(z):
        return (z % 8) * 2 + z // 8

    return lax.ppermute(
        value, ("zl", "zh"), [(place((z + step) % 16), place(z)) for z in range(16)]
    )


def contract_last(left_side, right_side):
    return lax.dot_general(
        left_side, right_side, (((1,), (1,)), ((), ())), preferred_element_type=jnp.float32
    )


def ordered(first, own, other):
    return jnp.where(first, own, other), jnp.where(first, other, own)


def after(value, earlier):
    return lax.optimization_barrier((value, earlier))[0]


def left_kernel(core_ref, normed_ref, own_ref, other_ref, left_ref):
    first = core_ref[0] == 0
    rank = left_ref.shape[0]
    total = jnp.zeros(left_ref.shape, jnp.float32)
    for pair in range(32):
        y, z = divmod(pair, 8)
        own = own_ref[y, z * rank : (z + 1) * rank]
        other = other_ref[y, z * rank : (z + 1) * rank]
        factor = jnp.concatenate(ordered(first, own, other), 1)
        total += contract_last(factor, normed_ref[:, pair * 256 : (pair + 1) * 256])
    left_ref[...] = total


def joined_kernel(*refs):
    out_ref = refs[-1]
    start = 0
    for ref in refs[:-1]:
        out_ref[start : start + ref.shape[0]] = ref[...]
        start += ref.shape[0]


def along_z_kernel(near_ref, ahead_ref, behind_ref, out_ref):
    three = 3 * BLOCK
    out_ref[:three] = near_ref[...]
    out_ref[three : 2 * three] = ahead_ref[...]
    out_ref[2 * three :] = behind_ref[BLOCK:]


def layer_kernel(
    place_ref, hidden_hbm, gain_ref, scale_ref, grad_ref, weight_hbm,
    values_ref, hidden_grad_ref, held, base, hidden_ref, arrived,
):
    chunks, depth = held.shape[:2]
    width = hidden_ref.shape[1]
    copies = [
        pltpu.make_async_copy(
            weight_hbm.at[pl.ds((chunk * 4 + part) * depth, depth)],
            held.at[chunk, :, pl.ds(part * BLOCK, BLOCK)],
            arrived.at[chunk * 4 + part],
        )
        for chunk in range(chunks)
        for part in range(4)
    ]
    hidden_copy = pltpu.make_async_copy(hidden_hbm, hidden_ref, arrived.at[4 * chunks])
    hidden_copy.start()
    for copy in copies:
        copy.start()
    grad = grad_ref[...]
    inv_rms = scale_ref[...]
    total = jnp.zeros(values_ref.shape, jnp.float32)
    hidden_copy.wait()
    for y in range(chunks // 2):
        for copy in copies[8 * y : 8 * y + 8]:
            copy.wait()
        for step in range(depth // BLOCK):
            rows = slice(step * BLOCK, (step + 1) * BLOCK)
            weight = jnp.concatenate([held[2 * y, rows], held[2 * y + 1, rows]], 0)
            offset = pl.multiple_of(y * (width // 4) + place_ref[step] * 256, 256)
            where = pl.ds(offset, 256)
            wide = hidden_ref[:, where].astype(jnp.float32)
            normed = (wide * inv_rms * gain_ref[:, where]).astype(jnp.bfloat16)
            total += jnp.dot(normed, weight, preferred_element_type=jnp.float32)
            base[:, where] = inv_rms * (contract_last(grad, weight) * gain_ref[:, where])
    values_ref[...] = total.astype(jnp.bfloat16)
    along = jnp.sum(total * grad.astype(jnp.float32), axis=1, keepdims=True)
    pull = inv_rms * inv_rms * along / width
    for start in range(0, width, 512):
        where = slice(start, start + 512)
        wide = hidden_ref[:, where].astype(jnp.float32)
        hidden_grad_ref[:, where] = (base[:, where] - wide * pull).astype(jnp.bfloat16)


def score_kernel(index_ref, docs_ref, here_ref, one_ref, two_ref, three_ref, scores_ref):
    lane = lax.broadcasted_iota(jnp.int32, docs_ref.shape[1:], 1)
    low = lane < docs_ref.shape[2] // 2
    pieces = []
    for pair in range(docs_ref.shape[0] // 2):
        even = docs_ref[2 * pair].astype(jnp.float32)
        odd = docs_ref[2 * pair + 1].astype(jnp.float32)
        pieces.append(jnp.where(low, even, odd).astype(jnp.bfloat16))
    docs = jnp.concatenate(pieces, 1)
    found = [contract_last(docs, ref[...]) for ref in (here_ref, one_ref, two_ref, three_ref)]
    size = here_ref.shape[0] // 2
    mine = [piece[:, :size] for piece in found]
    others = [piece[:, size:] for piece in found]
    zh, x = index_ref[0], index_ref[1]
    result = jnp.zeros(scores_ref.shape, jnp.float32)
    for turn in range(4):
        order = [(place - turn) % 4 for place in range(4)]
        one_half = [mine[step] for step in order]
        other_half = [others[step] for step in order]
        for side, parts in ((0, one_half + other_half), (1, other_half + one_half)):
            chosen = jnp.logical_and(zh == side, x == turn)
            result = jnp.where(chosen, jnp.concatenate(parts, 1), result)
    scores_ref[...] = result


def call(body, out_shape, scalars, name, limit=LIMIT):
    def run(*operands):
        smem = pl.BlockSpec(memory_space=pltpu.SMEM)
        vmem = pl.BlockSpec(memory_space=pltpu.VMEM)
        return pl.pallas_call(
            body,
            out_shape=out_shape,
            in_specs=[smem] * scalars + [vmem] * (len(operands) - scalars),
            out_specs=jax.tree.map(lambda _: vmem, out_shape),
            compiler_params=pltpu.CompilerParams(vmem_limit_bytes=limit),
            name=name,
        )(*operands)

    return run


def from_x(value, step):
    return lax.ppermute(value, "x", [((x + step) % 4, x) for x in range(4)])


def struct(shape, dtype):
    return jax.ShapeDtypeStruct(shape, dtype)


def shards(
    hidden_in, norm_gain, value_weight, input_proj, value_grad, output_proj, doc_ids, queries
):
    rows, width = hidden_in.shape
    kv = value_weight.shape[1]
    rank = input_proj.shape[1]
    core = lax.axis_index("core")
    core_row = core.astype(jnp.int32).reshape(1)
    on_first = core == 0

    quarter = lax.dynamic_slice_in_dim(value_weight, lax.axis_index("x") * BLOCK, BLOCK, 1)
    ahead, behind = from_z(quarter, 1), from_z(quarter, -1)
    near = call(joined_kernel, struct((3 * BLOCK, BLOCK), jnp.bfloat16), 0, "near_three")(
        behind, quarter, ahead
    )
    far_ahead, far_behind = from_z(near, 3), from_z(near, -3)

    factor = input_proj.T.reshape(4, 8, 2, BLOCK).transpose(0, 2, 1, 3).reshape(rank, BLOCK)
    right_t = lax.dot_general(
        output_proj, value_grad, (((0,), (1,)), ((), ())), preferred_element_type=jnp.float32
    ).astype(jnp.bfloat16)
    ids_rows = jnp.broadcast_to(doc_ids.astype(jnp.bfloat16)[None], (16, rows))
    factor_z = spread_to_all(after(factor, near), "zl").reshape(-1, BLOCK)
    packed = spread_to_all(jnp.concatenate([factor_z, right_t, ids_rows], 0), "y")
    packed_other = swapped(packed, "core")
    q_other = swapped(after(queries, factor_z), "zh")
    packed_other, q_other = lax.optimization_barrier((packed_other, q_other))

    wide_in = hidden_in.astype(jnp.float32)
    inv_rms = lax.rsqrt(jnp.mean(wide_in * wide_in, axis=1, keepdims=True) + EPSILON)
    normed = (wide_in * inv_rms * norm_gain).astype(jnp.bfloat16)
    left_t = call(left_kernel, struct((rank, rows), jnp.float32), 1, "left_factor")(
        core_row, normed, packed, packed_other
    )

    w_z = call(along_z_kernel, struct((8 * BLOCK, BLOCK), jnp.bfloat16), 0, "along_z")(
        near, *after((far_ahead, far_behind), factor_z)
    )
    w_all = lax.all_gather(w_z, ("y", "core", "x"), axis=0, tiled=True)
    z_place = (lax.axis_index("zl") + jnp.array(Z_STEPS, jnp.int32)) % 8


    left_all = lax.all_to_all(
        left_t.reshape(8, rank // 8, rows), ("y", "core"), 0, 0, tiled=True
    )

    base = 8 * rank
    tail = jnp.stack(ordered(on_first, packed[:, base:], packed_other[:, base:]), 1)
    tail = tail.reshape(8, -1, rows).astype(jnp.float32)
    right_flat = tail[:, :rank].transpose(1, 0, 2).reshape(rank, -1)
    ids_all = tail[:, rank].reshape(1, -1)
    left_flat = left_all.transpose(1, 0, 2).reshape(8, 1, -1)
    doc_count = 64
    doc_range = jnp.arange(doc_count, dtype=jnp.float32)[:, None]
    onehot = (ids_all == doc_range).astype(jnp.float32)
    spread = (onehot[None] * left_flat).reshape(8 * doc_count, -1)
    doc_term = lax.dot_general(
        spread, right_flat, (((1,), (1,)), ((), ())), precision=lax.Precision.HIGHEST
    )
    doc_parts = lax.all_to_all(
        doc_term.reshape(64, 8, rank), ("zl", "zh", "x"), 0, 0, tiled=True
    )
    q_here = after(jnp.concatenate([queries, q_other], 0), doc_term)
    q_turns = [from_x(q_here, step) for step in (1, 2, 3)]
    own_docs = jnp.sum(doc_parts, 0).astype(jnp.bfloat16)
    doc_low = spread_to_all(jnp.concatenate([own_docs, own_docs], 1), DP)

    vmem = pl.BlockSpec(memory_space=pltpu.VMEM)
    hbm = pl.BlockSpec(memory_space=pltpu.HBM)
    chunks = 8
    values_out, hidden_grad = pl.pallas_call(
        layer_kernel,
        out_shape=(struct((rows, kv), jnp.bfloat16), struct((rows, width), jnp.bfloat16)),
        in_specs=[pl.BlockSpec(memory_space=pltpu.SMEM), hbm, vmem, vmem, vmem, hbm],
        out_specs=(vmem, vmem),
        scratch_shapes=[
            pltpu.VMEM((chunks, width // chunks, kv), jnp.bfloat16),
            pltpu.VMEM((rows, width), jnp.float32),
            pltpu.VMEM((rows, width), jnp.bfloat16),
            pltpu.SemaphoreType.DMA((4 * chunks + 1,)),
        ],
        compiler_params=pltpu.CompilerParams(vmem_limit_bytes=58 * 1024 * 1024),
        name="layer",
    )(
        z_place.astype(jnp.int32), hidden_in, norm_gain.reshape(1, width), inv_rms,
        value_grad, w_all,
    )
    doc_low, values_out = lax.optimization_barrier((doc_low, values_out))
    score_index = jnp.stack([lax.axis_index("zh"), lax.axis_index("x")]).astype(jnp.int32)
    scores = call(score_kernel, struct((8, 8 * queries.shape[0]), jnp.float32), 1, "scores")(
        score_index, doc_low, q_here, *q_turns
    )
    return (values_out, hidden_grad, scores)


def solution(mesh):
    fine = Mesh(mesh.devices.reshape(4, 8, 2, 2, 4), DP + SCORE)
    tokens = SCORE + DP
    placed = (
        P(tokens, None),
        P(),
        P(DP, None),
        P(DP, None),
        P(tokens, None),
        P(),
        P(tokens),
        P(DP + SCORE, None),
    )
    return jax.shard_map(
        shards,
        mesh=fine,
        in_specs=placed,
        out_specs=(P(tokens, None), P(tokens, None), P(SCORE, DP)),
        check_vma=False,
    )
```

```python
import jax
import jax.numpy as jnp
from jax import lax
from jax.experimental import pallas as pl
from jax.experimental.pallas import tpu as pltpu
from jax.sharding import Mesh
from jax.sharding import PartitionSpec as P

EPSILON = 1e-05
DP = ("y", "zl", "core")
SCORE = ("zh", "x")
Z_STEPS = (-1, 0, 1, 2, 3, 4, -3, -2)
BLOCK = 128
LIMIT = 16 * 1024 * 1024


def spread_to_all(value, axes):
    count = lax.axis_size(axes)
    copies = jnp.broadcast_to(value[None], (count,) + value.shape)
    return lax.all_to_all(copies, axes, 0, 0, tiled=True)


def swapped(value, axis):
    return lax.ppermute(value, axis, [(0, 1), (1, 0)])


def from_z(value, step):
    def place(z):
        return (z % 8) * 2 + z // 8

    return lax.ppermute(
        value, ("zl", "zh"), [(place((z + step) % 16), place(z)) for z in range(16)]
    )


def contract_last(left_side, right_side):
    return lax.dot_general(
        left_side, right_side, (((1,), (1,)), ((), ())), preferred_element_type=jnp.float32
    )


def ordered(first, own, other):
    return jnp.where(first, own, other), jnp.where(first, other, own)


def after(value, earlier):
    return lax.optimization_barrier((value, earlier))[0]


def left_kernel(core_ref, normed_ref, own_ref, other_ref, left_ref):
    first = core_ref[0] == 0
    rank = left_ref.shape[0]
    total = jnp.zeros(left_ref.shape, jnp.float32)
    for pair in range(32):
        y, z = divmod(pair, 8)
        own = own_ref[y, z * rank : (z + 1) * rank]
        other = other_ref[y, z * rank : (z + 1) * rank]
        factor = jnp.concatenate(ordered(first, own, other), 1)
        total += contract_last(factor, normed_ref[:, pair * 256 : (pair + 1) * 256])
    left_ref[...] = total


def joined_kernel(*refs):
    out_ref = refs[-1]
    start = 0
    for ref in refs[:-1]:
        out_ref[start : start + ref.shape[0]] = ref[...]
        start += ref.shape[0]


def along_z_kernel(near_ref, ahead_ref, behind_ref, out_ref):
    three = 3 * BLOCK
    out_ref[:three] = near_ref[...]
    out_ref[three : 2 * three] = ahead_ref[...]
    out_ref[2 * three :] = behind_ref[BLOCK:]


def layer_kernel(
    place_ref, hidden_hbm, gain_ref, scale_ref, grad_ref, weight_hbm,
    values_ref, hidden_grad_ref, held, base, hidden_ref, arrived,
):
    chunks, depth = held.shape[:2]
    width = hidden_ref.shape[1]
    copies = [
        pltpu.make_async_copy(
            weight_hbm.at[pl.ds((chunk * 4 + part) * depth, depth)],
            held.at[chunk, :, pl.ds(part * BLOCK, BLOCK)],
            arrived.at[chunk * 4 + part],
        )
        for chunk in range(chunks)
        for part in range(4)
    ]
    hidden_copy = pltpu.make_async_copy(hidden_hbm, hidden_ref, arrived.at[4 * chunks])
    hidden_copy.start()
    for copy in copies:
        copy.start()
    grad = grad_ref[...]
    inv_rms = scale_ref[...]
    total = jnp.zeros(values_ref.shape, jnp.float32)
    hidden_copy.wait()
    for y in range(chunks // 2):
        for copy in copies[8 * y : 8 * y + 8]:
            copy.wait()
        for step in range(depth // BLOCK):
            rows = slice(step * BLOCK, (step + 1) * BLOCK)
            weight = jnp.concatenate([held[2 * y, rows], held[2 * y + 1, rows]], 0)
            offset = pl.multiple_of(y * (width // 4) + place_ref[step] * 256, 256)
            where = pl.ds(offset, 256)
            wide = hidden_ref[:, where].astype(jnp.float32)
            normed = (wide * inv_rms * gain_ref[:, where]).astype(jnp.bfloat16)
            total += jnp.dot(normed, weight, preferred_element_type=jnp.float32)
            base[:, where] = inv_rms * (contract_last(grad, weight) * gain_ref[:, where])
    values_ref[...] = total.astype(jnp.bfloat16)
    along = jnp.sum(total * grad.astype(jnp.float32), axis=1, keepdims=True)
    pull = inv_rms * inv_rms * along / width
    for start in range(0, width, 512):
        where = slice(start, start + 512)
        wide = hidden_ref[:, where].astype(jnp.float32)
        hidden_grad_ref[:, where] = (base[:, where] - wide * pull).astype(jnp.bfloat16)


def score_kernel(index_ref, docs_ref, here_ref, one_ref, two_ref, three_ref, scores_ref):
    lane = lax.broadcasted_iota(jnp.int32, docs_ref.shape[1:], 1)
    low = lane < docs_ref.shape[2] // 2
    pieces = []
    for pair in range(docs_ref.shape[0] // 2):
        even = docs_ref[2 * pair].astype(jnp.float32)
        odd = docs_ref[2 * pair + 1].astype(jnp.float32)
        pieces.append(jnp.where(low, even, odd).astype(jnp.bfloat16))
    docs = jnp.concatenate(pieces, 1)
    found = [contract_last(docs, ref[...]) for ref in (here_ref, one_ref, two_ref, three_ref)]
    size = here_ref.shape[0] // 2
    mine = [piece[:, :size] for piece in found]
    others = [piece[:, size:] for piece in found]
    zh, x = index_ref[0], index_ref[1]
    result = jnp.zeros(scores_ref.shape, jnp.float32)
    for turn in range(4):
        order = [(place - turn) % 4 for place in range(4)]
        one_half = [mine[step] for step in order]
        other_half = [others[step] for step in order]
        for side, parts in ((0, one_half + other_half), (1, other_half + one_half)):
            chosen = jnp.logical_and(zh == side, x == turn)
            result = jnp.where(chosen, jnp.concatenate(parts, 1), result)
    scores_ref[...] = result


def call(body, out_shape, scalars, name, limit=LIMIT):
    def run(*operands):
        smem = pl.BlockSpec(memory_space=pltpu.SMEM)
        vmem = pl.BlockSpec(memory_space=pltpu.VMEM)
        return pl.pallas_call(
            body,
            out_shape=out_shape,
            in_specs=[smem] * scalars + [vmem] * (len(operands) - scalars),
            out_specs=jax.tree.map(lambda _: vmem, out_shape),
            compiler_params=pltpu.CompilerParams(vmem_limit_bytes=limit),
            name=name,
        )(*operands)

    return run


def from_x(value, step):
    return lax.ppermute(value, "x", [((x + step) % 4, x) for x in range(4)])


def struct(shape, dtype):
    return jax.ShapeDtypeStruct(shape, dtype)


def shards(
    hidden_in, norm_gain, value_weight, input_proj, value_grad, output_proj, doc_ids, queries
):
    rows, width = hidden_in.shape
    kv = value_weight.shape[1]
    rank = input_proj.shape[1]
    core = lax.axis_index("core")
    core_row = core.astype(jnp.int32).reshape(1)
    on_first = core == 0

    factor = input_proj.T.reshape(4, 8, 2, BLOCK).transpose(0, 2, 1, 3).reshape(rank, BLOCK)
    right_t = lax.dot_general(
        output_proj, value_grad, (((0,), (1,)), ((), ())), preferred_element_type=jnp.float32
    ).astype(jnp.bfloat16)
    ids_rows = jnp.broadcast_to(doc_ids.astype(jnp.bfloat16)[None], (16, rows))
    factor_z = spread_to_all(factor, "zl").reshape(-1, BLOCK)
    packed = spread_to_all(jnp.concatenate([factor_z, right_t, ids_rows], 0), "y")
    packed_other = swapped(packed, "core")

    quarter = lax.dynamic_slice_in_dim(value_weight, lax.axis_index("x") * BLOCK, BLOCK, 1)
    ahead, behind = from_z(quarter, 1), from_z(quarter, -1)
    near = call(joined_kernel, struct((3 * BLOCK, BLOCK), jnp.bfloat16), 0, "near_three")(
        behind, quarter, ahead
    )
    near = after(near, factor_z)
    far_ahead, far_behind = from_z(near, 3), from_z(near, -3)

    wide_in = hidden_in.astype(jnp.float32)
    inv_rms = lax.rsqrt(jnp.mean(wide_in * wide_in, axis=1, keepdims=True) + EPSILON)
    normed = (wide_in * inv_rms * norm_gain).astype(jnp.bfloat16)
    left_t = call(left_kernel, struct((rank, rows), jnp.float32), 1, "left_factor")(
        core_row, normed, packed, packed_other
    )

    w_z = call(along_z_kernel, struct((8 * BLOCK, BLOCK), jnp.bfloat16), 0, "along_z")(
        near, *after((far_ahead, far_behind), left_t)
    )
    w_all = lax.all_gather(w_z, ("y", "core", "x"), axis=0, tiled=True)
    z_place = (lax.axis_index("zl") + jnp.array(Z_STEPS, jnp.int32)) % 8

    q_other = swapped(after(queries, left_t), "zh")

    left_all = lax.all_to_all(
        left_t.reshape(8, rank // 8, rows), ("y", "core"), 0, 0, tiled=True
    )

    base = 8 * rank
    tail = jnp.stack(ordered(on_first, packed[:, base:], packed_other[:, base:]), 1)
    tail = tail.reshape(8, -1, rows).astype(jnp.float32)
    right_flat = tail[:, :rank].transpose(1, 0, 2).reshape(rank, -1)
    ids_all = tail[:, rank].reshape(1, -1)
    left_flat = left_all.transpose(1, 0, 2).reshape(8, 1, -1)
    doc_count = 64
    doc_range = jnp.arange(doc_count, dtype=jnp.float32)[:, None]
    onehot = (ids_all == doc_range).astype(jnp.float32)
    spread = (onehot[None] * left_flat).reshape(8 * doc_count, -1)
    doc_term = lax.dot_general(
        spread, right_flat, (((1,), (1,)), ((), ())), precision=lax.Precision.HIGHEST
    )
    doc_parts = lax.all_to_all(
        doc_term.reshape(64, 8, rank), ("zl", "zh", "x"), 0, 0, tiled=True
    )
    q_here = after(jnp.concatenate([queries, q_other], 0), doc_term)
    q_turns = [from_x(q_here, step) for step in (1, 2, 3)]
    own_docs = jnp.sum(doc_parts, 0).astype(jnp.bfloat16)
    doc_low = spread_to_all(jnp.concatenate([own_docs, own_docs], 1), DP)

    score_index = jnp.stack([lax.axis_index("zh"), lax.axis_index("x")]).astype(jnp.int32)
    scores = call(score_kernel, struct((8, 8 * queries.shape[0]), jnp.float32), 1, "scores")(
        score_index, doc_low, q_here, *q_turns
    )
    w_all = after(w_all, scores)

    vmem = pl.BlockSpec(memory_space=pltpu.VMEM)
    hbm = pl.BlockSpec(memory_space=pltpu.HBM)
    chunks = 8
    values_out, hidden_grad = pl.pallas_call(
        layer_kernel,
        out_shape=(struct((rows, kv), jnp.bfloat16), struct((rows, width), jnp.bfloat16)),
        in_specs=[pl.BlockSpec(memory_space=pltpu.SMEM), hbm, vmem, vmem, vmem, hbm],
        out_specs=(vmem, vmem),
        scratch_shapes=[
            pltpu.VMEM((chunks, width // chunks, kv), jnp.bfloat16),
            pltpu.VMEM((rows, width), jnp.float32),
            pltpu.VMEM((rows, width), jnp.bfloat16),
            pltpu.SemaphoreType.DMA((4 * chunks + 1,)),
        ],
        compiler_params=pltpu.CompilerParams(vmem_limit_bytes=58 * 1024 * 1024),
        name="layer",
    )(
        z_place.astype(jnp.int32), hidden_in, norm_gain.reshape(1, width), inv_rms,
        value_grad, w_all,
    )
    return (values_out, hidden_grad, scores)


def solution(mesh):
    fine = Mesh(mesh.devices.reshape(4, 8, 2, 2, 4), DP + SCORE)
    tokens = SCORE + DP
    placed = (
        P(tokens, None),
        P(),
        P(DP, None),
        P(DP, None),
        P(tokens, None),
        P(),
        P(tokens),
        P(DP + SCORE, None),
    )
    return jax.shard_map(
        shards,
        mesh=fine,
        in_specs=placed,
        out_specs=(P(tokens, None), P(tokens, None), P(SCORE, DP)),
        check_vma=False,
    )
```

```python
import jax
import jax.numpy as jnp
from jax import lax
from jax.experimental import pallas as pl
from jax.experimental.pallas import tpu as pltpu
from jax.sharding import Mesh
from jax.sharding import PartitionSpec as P

EPSILON = 1e-05
DP = ("y", "zl", "core")
SCORE = ("zh", "x")
Z_STEPS = (-1, 0, 1, 2, 3, 4, -3, -2)
BLOCK = 128
LIMIT = 16 * 1024 * 1024


def spread_to_all(value, axes):
    count = lax.axis_size(axes)
    copies = jnp.broadcast_to(value[None], (count,) + value.shape)
    return lax.all_to_all(copies, axes, 0, 0, tiled=True)


def swapped(value, axis):
    return lax.ppermute(value, axis, [(0, 1), (1, 0)])


def from_z(value, step):
    def place(z):
        return (z % 8) * 2 + z // 8

    return lax.ppermute(
        value, ("zl", "zh"), [(place((z + step) % 16), place(z)) for z in range(16)]
    )


def contract_last(left_side, right_side):
    return lax.dot_general(
        left_side, right_side, (((1,), (1,)), ((), ())), preferred_element_type=jnp.float32
    )


def ordered(first, own, other):
    return jnp.where(first, own, other), jnp.where(first, other, own)


def after(value, earlier):
    return lax.optimization_barrier((value, earlier))[0]


def left_kernel(core_ref, normed_ref, own_ref, other_ref, left_ref):
    first = core_ref[0] == 0
    rank = left_ref.shape[0]
    total = jnp.zeros(left_ref.shape, jnp.float32)
    for pair in range(32):
        y, z = divmod(pair, 8)
        own = own_ref[y, z * rank : (z + 1) * rank]
        other = other_ref[y, z * rank : (z + 1) * rank]
        factor = jnp.concatenate(ordered(first, own, other), 1)
        total += contract_last(factor, normed_ref[:, pair * 256 : (pair + 1) * 256])
    left_ref[...] = total


def joined_kernel(*refs):
    out_ref = refs[-1]
    start = 0
    for ref in refs[:-1]:
        out_ref[start : start + ref.shape[0]] = ref[...]
        start += ref.shape[0]


def along_z_kernel(near_ref, ahead_ref, behind_ref, out_ref):
    three = 3 * BLOCK
    out_ref[:three] = near_ref[...]
    out_ref[three : 2 * three] = ahead_ref[...]
    out_ref[2 * three :] = behind_ref[BLOCK:]


def layer_kernel(
    place_ref, hidden_hbm, gain_ref, scale_ref, grad_ref, weight_hbm,
    values_ref, hidden_grad_ref, held, base, hidden_ref, arrived,
):
    chunks, depth = held.shape[:2]
    width = hidden_ref.shape[1]
    copies = [
        pltpu.make_async_copy(
            weight_hbm.at[pl.ds((chunk // 2 * 8 + part * 2 + chunk % 2) * depth, depth)],
            held.at[chunk, :, pl.ds(part * BLOCK, BLOCK)],
            arrived.at[chunk * 4 + part],
        )
        for chunk in range(chunks)
        for part in range(4)
    ]
    hidden_copy = pltpu.make_async_copy(hidden_hbm, hidden_ref, arrived.at[4 * chunks])
    hidden_copy.start()
    for copy in copies:
        copy.start()
    grad = grad_ref[...]
    inv_rms = scale_ref[...]
    total = jnp.zeros(values_ref.shape, jnp.float32)
    hidden_copy.wait()
    for y in range(chunks // 2):
        for copy in copies[8 * y : 8 * y + 8]:
            copy.wait()
        for step in range(depth // BLOCK):
            rows = slice(step * BLOCK, (step + 1) * BLOCK)
            weight = jnp.concatenate([held[2 * y, rows], held[2 * y + 1, rows]], 0)
            offset = pl.multiple_of(y * (width // 4) + place_ref[step] * 256, 256)
            where = pl.ds(offset, 256)
            wide = hidden_ref[:, where].astype(jnp.float32)
            normed = (wide * inv_rms * gain_ref[:, where]).astype(jnp.bfloat16)
            total += jnp.dot(normed, weight, preferred_element_type=jnp.float32)
            base[:, where] = inv_rms * (contract_last(grad, weight) * gain_ref[:, where])
    values_ref[...] = total.astype(jnp.bfloat16)
    along = jnp.sum(total * grad.astype(jnp.float32), axis=1, keepdims=True)
    pull = inv_rms * inv_rms * along / width
    for start in range(0, width, 512):
        where = slice(start, start + 512)
        wide = hidden_ref[:, where].astype(jnp.float32)
        hidden_grad_ref[:, where] = (base[:, where] - wide * pull).astype(jnp.bfloat16)


def score_kernel(index_ref, docs_ref, here_ref, one_ref, two_ref, three_ref, scores_ref):
    lane = lax.broadcasted_iota(jnp.int32, docs_ref.shape[1:], 1)
    low = lane < docs_ref.shape[2] // 2
    pieces = []
    for pair in range(docs_ref.shape[0] // 2):
        even = docs_ref[2 * pair].astype(jnp.float32)
        odd = docs_ref[2 * pair + 1].astype(jnp.float32)
        pieces.append(jnp.where(low, even, odd).astype(jnp.bfloat16))
    docs = jnp.concatenate(pieces, 1)
    found = [contract_last(docs, ref[...]) for ref in (here_ref, one_ref, two_ref, three_ref)]
    size = here_ref.shape[0] // 2
    mine = [piece[:, :size] for piece in found]
    others = [piece[:, size:] for piece in found]
    zh, x = index_ref[0], index_ref[1]
    result = jnp.zeros(scores_ref.shape, jnp.float32)
    for turn in range(4):
        order = [(place - turn) % 4 for place in range(4)]
        one_half = [mine[step] for step in order]
        other_half = [others[step] for step in order]
        for side, parts in ((0, one_half + other_half), (1, other_half + one_half)):
            chosen = jnp.logical_and(zh == side, x == turn)
            result = jnp.where(chosen, jnp.concatenate(parts, 1), result)
    scores_ref[...] = result


def call(body, out_shape, scalars, name, limit=LIMIT):
    def run(*operands):
        smem = pl.BlockSpec(memory_space=pltpu.SMEM)
        vmem = pl.BlockSpec(memory_space=pltpu.VMEM)
        return pl.pallas_call(
            body,
            out_shape=out_shape,
            in_specs=[smem] * scalars + [vmem] * (len(operands) - scalars),
            out_specs=jax.tree.map(lambda _: vmem, out_shape),
            compiler_params=pltpu.CompilerParams(vmem_limit_bytes=limit),
            name=name,
        )(*operands)

    return run


def from_x(value, step):
    return lax.ppermute(value, "x", [((x + step) % 4, x) for x in range(4)])


def struct(shape, dtype):
    return jax.ShapeDtypeStruct(shape, dtype)


def shards(
    hidden_in, norm_gain, value_weight, input_proj, value_grad, output_proj, doc_ids, queries
):
    rows, width = hidden_in.shape
    kv = value_weight.shape[1]
    rank = input_proj.shape[1]
    core = lax.axis_index("core")
    core_row = core.astype(jnp.int32).reshape(1)
    on_first = core == 0

    factor = input_proj.T.reshape(4, 8, 2, BLOCK).transpose(0, 2, 1, 3).reshape(rank, BLOCK)
    right_t = lax.dot_general(
        output_proj, value_grad, (((0,), (1,)), ((), ())), preferred_element_type=jnp.float32
    ).astype(jnp.bfloat16)
    ids_rows = jnp.broadcast_to(doc_ids.astype(jnp.bfloat16)[None], (16, rows))
    factor_z = spread_to_all(factor, "zl").reshape(-1, BLOCK)
    packed = spread_to_all(jnp.concatenate([factor_z, right_t, ids_rows], 0), "y")
    packed_other = swapped(packed, "core")

    quarter = lax.dynamic_slice_in_dim(value_weight, lax.axis_index("x") * BLOCK, BLOCK, 1)
    ahead, behind = from_z(quarter, 1), from_z(quarter, -1)
    near = call(joined_kernel, struct((3 * BLOCK, BLOCK), jnp.bfloat16), 0, "near_three")(
        behind, quarter, ahead
    )
    near = after(near, factor_z)
    far_ahead, far_behind = from_z(near, 3), from_z(near, -3)

    wide_in = hidden_in.astype(jnp.float32)
    inv_rms = lax.rsqrt(jnp.mean(wide_in * wide_in, axis=1, keepdims=True) + EPSILON)
    normed = (wide_in * inv_rms * norm_gain).astype(jnp.bfloat16)
    left_t = call(left_kernel, struct((rank, rows), jnp.float32), 1, "left_factor")(
        core_row, normed, packed, packed_other
    )

    w_z = call(along_z_kernel, struct((8 * BLOCK, BLOCK), jnp.bfloat16), 0, "along_z")(
        near, *after((far_ahead, far_behind), left_t)
    )
    w_all = lax.all_gather(w_z, ("y", "x", "core"), axis=0, tiled=True)
    z_place = (lax.axis_index("zl") + jnp.array(Z_STEPS, jnp.int32)) % 8

    q_other = swapped(after(queries, left_t), "zh")

    left_all = lax.all_to_all(
        left_t.reshape(8, rank // 8, rows), ("y", "core"), 0, 0, tiled=True
    )

    base = 8 * rank
    tail = jnp.stack(ordered(on_first, packed[:, base:], packed_other[:, base:]), 1)
    tail = tail.reshape(8, -1, rows).astype(jnp.float32)
    right_flat = tail[:, :rank].transpose(1, 0, 2).reshape(rank, -1)
    ids_all = tail[:, rank].reshape(1, -1)
    left_flat = left_all.transpose(1, 0, 2).reshape(8, 1, -1)
    doc_count = 64
    doc_range = jnp.arange(doc_count, dtype=jnp.float32)[:, None]
    onehot = (ids_all == doc_range).astype(jnp.float32)
    spread = (onehot[None] * left_flat).reshape(8 * doc_count, -1)
    doc_term = lax.dot_general(
        spread, right_flat, (((1,), (1,)), ((), ())), precision=lax.Precision.HIGHEST
    )
    doc_parts = lax.all_to_all(
        doc_term.reshape(64, 8, rank), ("zl", "zh", "x"), 0, 0, tiled=True
    )
    q_here = after(jnp.concatenate([queries, q_other], 0), doc_term)
    q_turns = [from_x(q_here, step) for step in (1, 2, 3)]
    own_docs = jnp.sum(doc_parts, 0).astype(jnp.bfloat16)
    doc_low = spread_to_all(jnp.concatenate([own_docs, own_docs], 1), DP)

    vmem = pl.BlockSpec(memory_space=pltpu.VMEM)
    hbm = pl.BlockSpec(memory_space=pltpu.HBM)
    chunks = 8
    values_out, hidden_grad = pl.pallas_call(
        layer_kernel,
        out_shape=(struct((rows, kv), jnp.bfloat16), struct((rows, width), jnp.bfloat16)),
        in_specs=[pl.BlockSpec(memory_space=pltpu.SMEM), hbm, vmem, vmem, vmem, hbm],
        out_specs=(vmem, vmem),
        scratch_shapes=[
            pltpu.VMEM((chunks, width // chunks, kv), jnp.bfloat16),
            pltpu.VMEM((rows, width), jnp.float32),
            pltpu.VMEM((rows, width), jnp.bfloat16),
            pltpu.SemaphoreType.DMA((4 * chunks + 1,)),
        ],
        compiler_params=pltpu.CompilerParams(vmem_limit_bytes=58 * 1024 * 1024),
        name="layer",
    )(
        z_place.astype(jnp.int32), hidden_in, norm_gain.reshape(1, width), inv_rms,
        value_grad, w_all,
    )
    doc_low, values_out = lax.optimization_barrier((doc_low, values_out))
    score_index = jnp.stack([lax.axis_index("zh"), lax.axis_index("x")]).astype(jnp.int32)
    scores = call(score_kernel, struct((8, 8 * queries.shape[0]), jnp.float32), 1, "scores")(
        score_index, doc_low, q_here, *q_turns
    )
    return (values_out, hidden_grad, scores)


def solution(mesh):
    fine = Mesh(mesh.devices.reshape(4, 8, 2, 2, 4), DP + SCORE)
    tokens = SCORE + DP
    placed = (
        P(tokens, None),
        P(),
        P(DP, None),
        P(DP, None),
        P(tokens, None),
        P(),
        P(tokens),
        P(DP + SCORE, None),
    )
    return jax.shard_map(
        shards,
        mesh=fine,
        in_specs=placed,
        out_specs=(P(tokens, None), P(tokens, None), P(SCORE, DP)),
        check_vma=False,
    )
```

```python
import jax
import jax.numpy as jnp
from jax import lax
from jax.experimental import pallas as pl
from jax.experimental.pallas import tpu as pltpu
from jax.sharding import Mesh
from jax.sharding import PartitionSpec as P

EPSILON = 1e-05
DP = ("y", "zl", "core")
SCORE = ("zh", "x")
Z_STEPS = (-1, 0, 1, 2, 3, 4, -3, -2)
BLOCK = 128
LIMIT = 16 * 1024 * 1024


def spread_to_all(value, axes):
    count = lax.axis_size(axes)
    copies = jnp.broadcast_to(value[None], (count,) + value.shape)
    return lax.all_to_all(copies, axes, 0, 0, tiled=True)


def swapped(value, axis):
    return lax.ppermute(value, axis, [(0, 1), (1, 0)])


def from_z(value, step):
    def place(z):
        return (z % 8) * 2 + z // 8

    return lax.ppermute(
        value, ("zl", "zh"), [(place((z + step) % 16), place(z)) for z in range(16)]
    )


def contract_last(left_side, right_side):
    return lax.dot_general(
        left_side, right_side, (((1,), (1,)), ((), ())), preferred_element_type=jnp.float32
    )


def ordered(first, own, other):
    return jnp.where(first, own, other), jnp.where(first, other, own)


def after(value, earlier):
    return lax.optimization_barrier((value, earlier))[0]


def left_kernel(core_ref, normed_ref, own_ref, other_ref, left_ref):
    first = core_ref[0] == 0
    rank = left_ref.shape[0]
    total = jnp.zeros(left_ref.shape, jnp.float32)
    for pair in range(32):
        y, z = divmod(pair, 8)
        own = own_ref[y, z * rank : (z + 1) * rank]
        other = other_ref[y, z * rank : (z + 1) * rank]
        factor = jnp.concatenate(ordered(first, own, other), 1)
        total += contract_last(factor, normed_ref[:, pair * 256 : (pair + 1) * 256])
    left_ref[...] = total


def joined_kernel(*refs):
    out_ref = refs[-1]
    start = 0
    for ref in refs[:-1]:
        out_ref[start : start + ref.shape[0]] = ref[...]
        start += ref.shape[0]


def along_z_kernel(near_ref, ahead_ref, behind_ref, out_ref):
    three = 3 * BLOCK
    out_ref[:three] = near_ref[...]
    out_ref[three : 2 * three] = ahead_ref[...]
    out_ref[2 * three :] = behind_ref[BLOCK:]


def layer_kernel(
    place_ref, hidden_hbm, gain_ref, scale_ref, grad_ref, weight_hbm,
    values_ref, hidden_grad_hbm, held, base, hidden_ref, formed, arrived, left_for,
):
    chunks, depth = held.shape[:2]
    width = hidden_ref.shape[1]
    copies = [
        pltpu.make_async_copy(
            weight_hbm.at[pl.ds((chunk // 2 * 8 + part * 2 + chunk % 2) * depth, depth)],
            held.at[chunk, :, pl.ds(part * BLOCK, BLOCK)],
            arrived.at[chunk * 4 + part],
        )
        for chunk in range(chunks)
        for part in range(4)
    ]
    hidden_copy = pltpu.make_async_copy(hidden_hbm, hidden_ref, arrived.at[4 * chunks])
    hidden_copy.start()
    for copy in copies:
        copy.start()
    grad = grad_ref[...]
    inv_rms = scale_ref[...]
    total = jnp.zeros(values_ref.shape, jnp.float32)
    hidden_copy.wait()
    for y in range(chunks // 2):
        for copy in copies[8 * y : 8 * y + 8]:
            copy.wait()
        for step in range(depth // BLOCK):
            rows = slice(step * BLOCK, (step + 1) * BLOCK)
            weight = jnp.concatenate([held[2 * y, rows], held[2 * y + 1, rows]], 0)
            offset = pl.multiple_of(y * (width // 4) + place_ref[step] * 256, 256)
            where = pl.ds(offset, 256)
            wide = hidden_ref[:, where].astype(jnp.float32)
            normed = (wide * inv_rms * gain_ref[:, where]).astype(jnp.bfloat16)
            total += jnp.dot(normed, weight, preferred_element_type=jnp.float32)
            base[:, where] = inv_rms * (contract_last(grad, weight) * gain_ref[:, where])
    values_ref[...] = total.astype(jnp.bfloat16)
    along = jnp.sum(total * grad.astype(jnp.float32), axis=1, keepdims=True)
    pull = inv_rms * inv_rms * along / width
    sent = []
    for start in range(0, width, 1024):
        where = slice(start, start + 1024)
        wide = hidden_ref[:, where].astype(jnp.float32)
        formed[:, where] = (base[:, where] - wide * pull).astype(jnp.bfloat16)
        columns = pl.ds(start, 1024)
        sent.append(
            pltpu.make_async_copy(
                formed.at[:, columns], hidden_grad_hbm.at[:, columns], left_for.at[len(sent)]
            )
        )
        sent[-1].start()
    for copy in sent:
        copy.wait()


def score_kernel(index_ref, docs_ref, here_ref, one_ref, two_ref, three_ref, scores_ref):
    lane = lax.broadcasted_iota(jnp.int32, docs_ref.shape[1:], 1)
    low = lane < docs_ref.shape[2] // 2
    pieces = []
    for pair in range(docs_ref.shape[0] // 2):
        even = docs_ref[2 * pair].astype(jnp.float32)
        odd = docs_ref[2 * pair + 1].astype(jnp.float32)
        pieces.append(jnp.where(low, even, odd).astype(jnp.bfloat16))
    docs = jnp.concatenate(pieces, 1)
    found = [contract_last(docs, ref[...]) for ref in (here_ref, one_ref, two_ref, three_ref)]
    size = here_ref.shape[0] // 2
    mine = [piece[:, :size] for piece in found]
    others = [piece[:, size:] for piece in found]
    zh, x = index_ref[0], index_ref[1]
    result = jnp.zeros(scores_ref.shape, jnp.float32)
    for turn in range(4):
        order = [(place - turn) % 4 for place in range(4)]
        one_half = [mine[step] for step in order]
        other_half = [others[step] for step in order]
        for side, parts in ((0, one_half + other_half), (1, other_half + one_half)):
            chosen = jnp.logical_and(zh == side, x == turn)
            result = jnp.where(chosen, jnp.concatenate(parts, 1), result)
    scores_ref[...] = result


def call(body, out_shape, scalars, name, limit=LIMIT):
    def run(*operands):
        smem = pl.BlockSpec(memory_space=pltpu.SMEM)
        vmem = pl.BlockSpec(memory_space=pltpu.VMEM)
        return pl.pallas_call(
            body,
            out_shape=out_shape,
            in_specs=[smem] * scalars + [vmem] * (len(operands) - scalars),
            out_specs=jax.tree.map(lambda _: vmem, out_shape),
            compiler_params=pltpu.CompilerParams(vmem_limit_bytes=limit),
            name=name,
        )(*operands)

    return run


def from_x(value, step):
    return lax.ppermute(value, "x", [((x + step) % 4, x) for x in range(4)])


def struct(shape, dtype):
    return jax.ShapeDtypeStruct(shape, dtype)


def shards(
    hidden_in, norm_gain, value_weight, input_proj, value_grad, output_proj, doc_ids, queries
):
    rows, width = hidden_in.shape
    kv = value_weight.shape[1]
    rank = input_proj.shape[1]
    core = lax.axis_index("core")
    core_row = core.astype(jnp.int32).reshape(1)
    on_first = core == 0

    factor = input_proj.T.reshape(4, 8, 2, BLOCK).transpose(0, 2, 1, 3).reshape(rank, BLOCK)
    right_t = lax.dot_general(
        output_proj, value_grad, (((0,), (1,)), ((), ())), preferred_element_type=jnp.float32
    ).astype(jnp.bfloat16)
    ids_rows = jnp.broadcast_to(doc_ids.astype(jnp.bfloat16)[None], (16, rows))
    factor_z = spread_to_all(factor, "zl").reshape(-1, BLOCK)
    packed = spread_to_all(jnp.concatenate([factor_z, right_t, ids_rows], 0), "y")
    packed_other = swapped(packed, "core")

    quarter = lax.dynamic_slice_in_dim(value_weight, lax.axis_index("x") * BLOCK, BLOCK, 1)
    ahead, behind = from_z(quarter, 1), from_z(quarter, -1)
    near = call(joined_kernel, struct((3 * BLOCK, BLOCK), jnp.bfloat16), 0, "near_three")(
        behind, quarter, ahead
    )
    near = after(near, factor_z)
    far_ahead, far_behind = from_z(near, 3), from_z(near, -3)

    wide_in = hidden_in.astype(jnp.float32)
    inv_rms = lax.rsqrt(jnp.mean(wide_in * wide_in, axis=1, keepdims=True) + EPSILON)
    normed = (wide_in * inv_rms * norm_gain).astype(jnp.bfloat16)
    left_t = call(left_kernel, struct((rank, rows), jnp.float32), 1, "left_factor")(
        core_row, normed, packed, packed_other
    )

    w_z = call(along_z_kernel, struct((8 * BLOCK, BLOCK), jnp.bfloat16), 0, "along_z")(
        near, *after((far_ahead, far_behind), left_t)
    )
    w_all = lax.all_gather(w_z, ("y", "x", "core"), axis=0, tiled=True)
    z_place = (lax.axis_index("zl") + jnp.array(Z_STEPS, jnp.int32)) % 8

    q_other = swapped(after(queries, left_t), "zh")

    left_all = lax.all_to_all(
        left_t.reshape(8, rank // 8, rows), ("y", "core"), 0, 0, tiled=True
    )

    base = 8 * rank
    tail = jnp.stack(ordered(on_first, packed[:, base:], packed_other[:, base:]), 1)
    tail = tail.reshape(8, -1, rows).astype(jnp.float32)
    right_flat = tail[:, :rank].transpose(1, 0, 2).reshape(rank, -1)
    ids_all = tail[:, rank].reshape(1, -1)
    left_flat = left_all.transpose(1, 0, 2).reshape(8, 1, -1)
    doc_count = 64
    doc_range = jnp.arange(doc_count, dtype=jnp.float32)[:, None]
    onehot = (ids_all == doc_range).astype(jnp.float32)
    spread = (onehot[None] * left_flat).reshape(8 * doc_count, -1)
    doc_term = lax.dot_general(
        spread, right_flat, (((1,), (1,)), ((), ())), precision=lax.Precision.HIGHEST
    )
    doc_parts = lax.all_to_all(
        doc_term.reshape(64, 8, rank), ("zl", "zh", "x"), 0, 0, tiled=True
    )
    q_here = after(jnp.concatenate([queries, q_other], 0), doc_term)
    q_turns = [from_x(q_here, step) for step in (1, 2, 3)]
    own_docs = jnp.sum(doc_parts, 0).astype(jnp.bfloat16)
    doc_low = spread_to_all(jnp.concatenate([own_docs, own_docs], 1), DP)

    vmem = pl.BlockSpec(memory_space=pltpu.VMEM)
    hbm = pl.BlockSpec(memory_space=pltpu.HBM)
    chunks = 8
    values_out, hidden_grad = pl.pallas_call(
        layer_kernel,
        out_shape=(struct((rows, kv), jnp.bfloat16), struct((rows, width), jnp.bfloat16)),
        in_specs=[pl.BlockSpec(memory_space=pltpu.SMEM), hbm, vmem, vmem, vmem, hbm],
        out_specs=(vmem, hbm),
        scratch_shapes=[
            pltpu.VMEM((chunks, width // chunks, kv), jnp.bfloat16),
            pltpu.VMEM((rows, width), jnp.float32),
            pltpu.VMEM((rows, width), jnp.bfloat16),
            pltpu.VMEM((rows, width), jnp.bfloat16),
            pltpu.SemaphoreType.DMA((4 * chunks + 1,)),
            pltpu.SemaphoreType.DMA((width // 1024,)),
        ],
        compiler_params=pltpu.CompilerParams(vmem_limit_bytes=58 * 1024 * 1024),
        name="layer",
    )(
        z_place.astype(jnp.int32), hidden_in, norm_gain.reshape(1, width), inv_rms,
        value_grad, w_all,
    )
    doc_low, values_out = lax.optimization_barrier((doc_low, values_out))
    score_index = jnp.stack([lax.axis_index("zh"), lax.axis_index("x")]).astype(jnp.int32)
    scores = call(score_kernel, struct((8, 8 * queries.shape[0]), jnp.float32), 1, "scores")(
        score_index, doc_low, q_here, *q_turns
    )
    return (values_out, hidden_grad, scores)


def solution(mesh):
    fine = Mesh(mesh.devices.reshape(4, 8, 2, 2, 4), DP + SCORE)
    tokens = SCORE + DP
    placed = (
        P(tokens, None),
        P(),
        P(DP, None),
        P(DP, None),
        P(tokens, None),
        P(),
        P(tokens),
        P(DP + SCORE, None),
    )
    return jax.shard_map(
        shards,
        mesh=fine,
        in_specs=placed,
        out_specs=(P(tokens, None), P(tokens, None), P(SCORE, DP)),
        check_vma=False,
    )
```
